512 devices in a mesh: depth: 32 (over x, y), image: 16 (over z, core).
Axes of the slice: x: 4, y: 8, z: 8, core: 2. Of those that a mesh axis runs over, the one named last changes fastest.
Arguments:
- bricks: bfloat16 [32, 4096, 16, 256], P('depth', 'image'), may hold values from -6 to 6
- cost: int32 [32, 4096], P('depth', 'image'), may hold values from 0 to 4, as said below
- order: int32 [2, 32], replicated, may hold values from 0 to 31, as said below
- color_gain: float32 [3], replicated, may hold values from 0.5 to 2
- color_bias: float32 [3], replicated, may hold values from -1 to 1
- ext_gain: float32 [1], replicated, may hold values from 0.6 to 1.4
- ext_bias: float32 [1], replicated, may hold values from -4.6 to -3.6
Outputs:
- frames: float32 [2, 4, 256, 4096], P(None, None, 'depth', 'image')
The draws below stay inside these ranges and needn't reach their ends.
Inputs may be any that keep to these rules, and one draw needn't show every extreme that they name: In each slab the 16 tiles hold together exactly 2048 bricks of cost above 0, and one tile of each slab has all 256 of its bricks nonempty. `order`: row v holds, for slab s, the bitwise exclusive or of s with a number m_v of 0 to 32 - 1 (the same for the whole row).
All inputs are finite; a program needn't handle non-finite values.
Results may differ from the reference program's by a relative error of at most 0.0003.
Values may be sent and summed in bfloat16 or wider, within the bound.
A program may use at most 128 MiB of HBM per device.

```python
import jax
import jax.numpy as jnp
from jax import lax

BE = 16
BC = 16
NB = 256
TR = 256
TC = 256
N_DEPTH = 32
N_IMAGE = 16


def draw_cost(key, part):

    def one_slab(slab_key):
        key_full, key_weight, key_perm, key_level = jax.random.split(slab_key, 4)
        places = jnp.arange(N_IMAGE, dtype=jnp.int32)
        full_tile = jax.random.randint(key_full, (), 0, N_IMAGE)
        weights = jax.random.randint(key_weight, (N_IMAGE,), 2, 5)
        weights = jnp.where(places == full_tile, 0, weights)
        spread_total = NB * (N_IMAGE // 2 - 1)
        shares = weights * spread_total // jnp.sum(weights)
        shortfall = spread_total - jnp.sum(shares)
        distance = (places - full_tile - 1) % N_IMAGE
        shares = shares + (distance < shortfall).astype(jnp.int32)
        counts = jnp.where(places == full_tile, NB, shares)
        perm_keys = jax.random.split(key_perm, N_IMAGE)
        ranks = jax.vmap(lambda one_key: jax.random.permutation(one_key, NB))(perm_keys)
        levels = jax.random.randint(key_level, (N_IMAGE, NB), 1, 5)
        return jnp.where(ranks < counts[:, None], levels, 0).reshape(N_IMAGE * NB)
    slab_keys = jax.random.split(jax.random.fold_in(key, 11), N_DEPTH)
    return jax.vmap(one_slab)(slab_keys).astype(jnp.int32)


def draw_order(key, part):
    masks = jax.random.randint(jax.random.fold_in(key, 23), (2, 1), 0, N_DEPTH).astype(jnp.int32)
    slab_index = jnp.arange(N_DEPTH, dtype=jnp.int32)[None, :]
    return jnp.bitwise_xor(slab_index, masks).astype(jnp.int32)


def block_scale(rng, shape, cuts, least, largest):
    def one(dim, parts):
        heights = jax.random.uniform(jax.random.fold_in(jax.random.fold_in(rng, 6), dim), (parts,), jnp.float32, least / len(cuts), largest / len(cuts))
        return jnp.repeat(jnp.exp(heights), shape[dim] // parts).reshape((-1,) + (1,) * (len(shape) - dim - 1))

    loudness = one(*cuts[0])
    for cut in cuts[1:]:
        loudness = loudness * one(*cut)
    return loudness


def bell_draw(stream_key, dims, width, bound, cuts=(), kind=jnp.bfloat16):
    drawn = jax.random.normal(stream_key, dims, jnp.float32) * width
    if len(cuts) > 0:
        drawn = block_scale(stream_key, dims, cuts, -0.22, 0.18) * drawn
    return jnp.clip(drawn, min=-bound, max=bound).astype(kind)


def setup_inputs(seed: int = 0) -> dict:
    key_list = jax.random.split(jax.random.key(seed), 8)
    bricks = bell_draw(key_list[0], (N_DEPTH, NB * N_IMAGE, BE, BE * BE), 1.0, 6.0, ((0, 32), (1, 16)))
    cost = draw_cost(jax.random.fold_in(key_list[7], 71), 0)
    order = draw_order(jax.random.fold_in(key_list[7], 71), 0)
    color_gain = jnp.clip(jax.random.uniform(key_list[3], (3,), jnp.float32, 0.5, 2.0), 0.5, 2.0)
    color_bias = jnp.clip(jax.random.uniform(key_list[4], (3,), jnp.float32, -1.0, 1.0), -1.0, 1.0)
    ext_gain = jnp.clip(jax.random.uniform(key_list[5], (1,), jnp.float32, 0.6, 1.4), 0.6, 1.4)
    ext_bias = jnp.clip(jax.random.uniform(key_list[6], (1,), jnp.float32, -4.6, -3.6), -4.6, -3.6)
    return {"bricks": bricks, "cost": cost, "order": order, "color_gain": color_gain, "color_bias": color_bias, "ext_gain": ext_gain, "ext_bias": ext_bias}


SHEAR = (0.45, -0.3)


def shear_taps(brick_edge, view):
    slice_index = jnp.arange(brick_edge, dtype=jnp.float32)[:, None]
    position = jnp.arange(brick_edge, dtype=jnp.float32)[None, :] + SHEAR[view] * (slice_index - (brick_edge - 1) / 2.0)
    anchor = jnp.floor(position)
    fraction = position - anchor
    weight_low = lax.optimization_barrier((1.0 - fraction).astype(jnp.bfloat16)).astype(jnp.float32)
    weight_high = lax.optimization_barrier(fraction.astype(jnp.bfloat16)).astype(jnp.float32)
    return anchor.astype(jnp.int32), weight_low, weight_high


def shade_samples(samples, levels, flip, color_gain, color_bias, ext_gain, ext_bias):
    brick_edge = samples.shape[1]
    slice_index = jnp.arange(brick_edge, dtype=jnp.int32)
    occupied = (slice_index[None, :] * 4 < levels[:, None] * brick_edge).astype(samples.dtype)[:, :, None]
    samples = jnp.where(flip, samples[:, ::-1], samples)
    occupied = jnp.where(flip, occupied[:, ::-1], occupied)
    extinction = jnp.exp(ext_gain[0] * samples + ext_bias[0])
    opacity = (1.0 - jnp.exp(-extinction)) * occupied
    remaining = jnp.cumprod(1.0 - opacity, axis=1)
    ahead_clear = jnp.concatenate([jnp.ones_like(remaining[:, :1]), remaining[:, :-1]], axis=1)
    weight = ahead_clear * opacity
    colors = [jnp.sum(weight * jax.nn.sigmoid(color_gain[channel] * samples + color_bias[channel]), axis=1) for channel in range(3)]
    return jnp.stack(colors + [1.0 - remaining[:, -1]], axis=1)


def sample_view(density, view):
    total_bricks, brick_edge, plane_size = density.shape
    voxels = density.reshape(total_bricks, brick_edge, brick_edge, brick_edge)
    anchor, weight_low, weight_high = shear_taps(brick_edge, view)

    def spread(table):
        if view == 0:
            return table[None, :, None, :]
        return table[None, :, :, None]

    def fetch_taps(indices):
        inside = ((indices >= 0) & (indices < brick_edge)).astype(density.dtype)
        clipped = jnp.clip(indices, 0, brick_edge - 1).astype(jnp.int32)
        values = jnp.take_along_axis(voxels, jnp.broadcast_to(spread(clipped), voxels.shape), axis=3 if view == 0 else 2)
        return values * spread(inside)

    samples = fetch_taps(anchor) * spread(weight_low) + fetch_taps(anchor + 1) * spread(weight_high)
    return samples.reshape(total_bricks, brick_edge, plane_size)


def arrange_tile(segments):
    brick_edge = BE
    rows = segments.shape[0] // BC
    tile_image = segments.reshape(rows, BC, 2, 4, brick_edge, brick_edge)
    tile_image = tile_image.transpose(2, 3, 0, 4, 1, 5)
    return tile_image.reshape(2, 4, rows * brick_edge, BC * brick_edge)


def composite(front_part, back_part):
    return front_part + (1.0 - front_part[..., 3:4, :, :]) * back_part


def reference(bricks, cost, order, color_gain, color_bias, ext_gain, ext_bias):
    flips = order[:, 0] > order[:, -1]
    by_rank = jnp.argsort(order, axis=1).astype(jnp.int32)
    zero_index = jnp.zeros((), jnp.int32)

    def one_tile(tile_number):
        offset = (tile_number * NB).astype(jnp.int32)

        def advance(totals, position):
            layers = []
            for view in range(2):
                slab_index = by_rank[view, position]
                density = lax.dynamic_slice(bricks, (slab_index, offset, zero_index, zero_index), (1, NB, BE, BE * BE))[0].astype(jnp.float32)
                levels = lax.dynamic_slice(cost, (slab_index, offset), (1, NB))[0]
                layers.append(shade_samples(sample_view(density, view), levels, flips[view], color_gain, color_bias, ext_gain, ext_bias))
            tile_image = arrange_tile(jnp.stack(layers, axis=1))
            return composite(totals, tile_image), None

        start = jnp.zeros((2, 4, TR, TC), jnp.float32)
        totals, unused = lax.scan(advance, start, jnp.arange(N_DEPTH, dtype=jnp.int32))
        return totals

    tiles = lax.map(one_tile, jnp.arange(N_IMAGE, dtype=jnp.int32))
    return tiles.transpose(1, 2, 3, 0, 4).reshape(2, 4, TR, N_IMAGE * TC)
```

```python
import jax
import jax.numpy as jnp
import numpy as np
import ml_dtypes
from jax import lax
from jax.experimental import pallas as pl
from jax.experimental.pallas import tpu as pltpu
from jax.sharding import PartitionSpec as P

BE = 16
PX = BE * BE
NB = 256
NX = 4
NY = 8
CHUNK = NB // NX
SHEAR = (0.45, -0.3)
LOG2E = 1.4426950408889634
TOP = 65535.0
MESH = pl.DeviceIdType.MESH


def shear_table():
    cells = np.arange(PX)
    rows, cols = cells // BE, cells % BE
    out = np.zeros((2, BE, PX, PX), np.float32)
    for view in range(2):
        k = np.arange(BE, dtype=np.float32)[:, None]
        position = np.arange(BE, dtype=np.float32)[None, :] + np.float32(SHEAR[view]) * (
            k - np.float32((BE - 1) / 2.0)
        )
        anchor = np.floor(position)
        fraction = (position - anchor).astype(np.float32)
        low = (np.float32(1.0) - fraction).astype(ml_dtypes.bfloat16).astype(np.float32)
        high = fraction.astype(ml_dtypes.bfloat16).astype(np.float32)
        anchor = anchor.astype(np.int32)
        along = cols if view == 0 else rows
        for tap, weight in ((0, low), (1, high)):
            source = anchor[:, along] + tap
            inside = (source >= 0) & (source < BE)
            for s in range(BE):
                index = (rows * BE + source[s]) if view == 0 else (source[s] * BE + cols)
                ok = inside[s]
                out[view, s, index[ok], cells[ok]] += weight[s, along][ok]
    return out.astype(ml_dtypes.bfloat16)


def encode(value):
    root = jnp.exp2(0.25 * jnp.log2(jnp.maximum(value, 1e-30)))
    code = jnp.minimum(root * TOP + 0.5, TOP).astype(jnp.int32) - 32768
    return code.astype(jnp.int16)


def decode(code):
    root = (code.astype(jnp.float32) + 32768.0) * (1.0 / TOP)
    square = root * root
    return square * square


def swap_rows_and_groups(block):
    row = lax.broadcasted_iota(jnp.int32, (8, 128), 0)
    group = lax.broadcasted_iota(jnp.int32, (8, 128), 1) // 16
    for bit in (1, 2, 4):
        row_bit = (row & bit) != 0
        group_bit = (group & bit) != 0
        from_below = pltpu.roll(pltpu.roll(block, 8 - bit, 0), 16 * bit, 1)
        from_above = pltpu.roll(pltpu.roll(block, bit, 0), 128 - 16 * bit, 1)
        moved = jnp.where(row_bit, from_above, from_below)
        block = jnp.where(row_bit == group_bit, block, moved)
    return block


def kernel(
    order, color_gain, color_bias, ext_gain, ext_bias, cost, bricks, table_hbm, out,
    raw, table, sliced, samples, levels, send, recv0, recv1, recv2, recv3, group,
    raw_sem, table_sem, send_sem, recv_sem, own_sem,
):
    me = lax.axis_index("depth")
    x, y = me // NY, me % NY

    def chunk_copy(i):
        c = lax.rem(x + i, NX)
        rows = pl.ds(pl.multiple_of(c * CHUNK * BE, CHUNK * BE), CHUNK * BE)
        return pltpu.make_async_copy(bricks.at[rows], raw.at[i], raw_sem.at[i])

    def table_copy(view):
        return pltpu.make_async_copy(table_hbm.at[view], table.at[view], table_sem.at[view])

    chunk_copy(0).start()
    table_copy(0).start()
    table_copy(1).start()
    for i in range(1, NX):
        chunk_copy(i).start()

    def peer(i, j):
        return lax.rem(x + i, NX) * NY + lax.rem(y + j, NY)

    barrier = pltpu.get_barrier_semaphore()

    def greet(t, carry):
        pl.semaphore_signal(barrier, inc=1, device_id={"depth": lax.rem(me + t, NX * NY)}, device_id_type=MESH)
        return carry

    lax.fori_loop(1, NX * NY, greet, 0)

    r = lax.broadcasted_iota(jnp.int32, (NB, NB), 0)
    q = lax.broadcasted_iota(jnp.int32, (NB, NB), 1)
    diagonal = jnp.where(r == q, (cost[...] * 4).astype(jnp.float32), 0.0).astype(jnp.bfloat16)
    levels[...] = jnp.dot(diagonal, jnp.ones((NB, 128), jnp.bfloat16), preferred_element_type=jnp.float32)
    regroup = jnp.where(q == (r % BE) * BE + r // BE, 1.0, 0.0).astype(jnp.bfloat16)

    masks = [order[v, 0] for v in range(2)]
    turned = [jnp.where(order[v, 0] > order[v, 31], 15, 0) for v in range(2)]
    gain = ext_gain[0] * LOG2E
    bias = ext_bias[0] * LOG2E + float(np.log2(LOG2E))
    half_gain = [color_gain[c] * 0.5 for c in range(3)]
    half_bias = [color_bias[c] * 0.5 for c in range(3)]

    recv = (recv0, recv1, recv2, recv3)

    def remote(i, j):
        slot = i * NY + j
        return pltpu.make_async_remote_copy(
            src_ref=send.at[slot], dst_ref=recv[i].at[j],
            send_sem=send_sem.at[slot], recv_sem=recv_sem.at[slot],
            device_id={"depth": peer(i, j)}, device_id_type=MESH,
        )

    def own_copy():
        return pltpu.make_async_copy(send.at[0], recv0.at[0], own_sem)

    def compute_chunk(i):
        chunk_copy(i).wait()
        for g in range(CHUNK // BE):
            lined = jnp.dot(
                regroup, raw[i, g * PX:(g + 1) * PX, :], preferred_element_type=jnp.float32
            ).astype(jnp.bfloat16)
            for k in range(BE):
                sliced[k, g * BE:(g + 1) * BE, :] = lined[k * BE:(k + 1) * BE, :]

        for view in range(2):
            if isinstance(i, int):
                table_copy(view).wait()

            def resample(k, carry):
                samples[view, k] = jnp.dot(
                    sliced[k], table[view, k], preferred_element_type=jnp.float32
                )
                return carry

            lax.fori_loop(0, BE, resample, 0, unroll=4)

        c = lax.rem(x + i, NX)
        for view in range(2):

            def shade(g, carry):
                rows = pl.ds(pl.multiple_of(g * BE, BE), BE)
                level = levels[pl.ds(pl.multiple_of(c * CHUNK + g * BE, BE), BE), :]
                level = jnp.concatenate([level, level], axis=1)
                depth = jnp.zeros((BE, PX), jnp.float32)
                clear = jnp.ones((BE, PX), jnp.float32)
                tints = [jnp.zeros((BE, PX), jnp.float32) for _ in range(3)]
                for k in range(BE):
                    kk = jnp.bitwise_xor(k, turned[view])
                    s = samples[view, kk, rows, :]
                    b = jnp.where(kk.astype(jnp.float32) < level, bias, -1e9)
                    depth = depth - jnp.exp2(s * gain + b)
                    after = jnp.exp2(depth)
                    weight = clear - after
                    clear = after
                    for ch in range(3):
                        tints[ch] = tints[ch] + weight * jnp.tanh(s * half_gain[ch] + half_bias[ch])
                opaque = 1.0 - clear
                values = [0.5 * (opaque + t) for t in tints] + [opaque]
                for ch in range(4):
                    code = encode(values[ch])
                    for h in range(2):
                        j = lax.rem(2 * g + h - y + NY, NY)
                        send[i * NY + j, view, ch] = code[:, h * 128:(h + 1) * 128]
                return carry

            lax.fori_loop(0, CHUNK // BE, shade, 0)

    def send_chunk(i, first):
        def go(j, carry):
            remote(i, j).start()
            return carry

        lax.fori_loop(first, NY, go, 0)

    compute_chunk(0)
    pl.semaphore_wait(barrier, NX * NY - 1)
    own_copy().start()
    send_chunk(0, 1)

    def later(i, carry):
        compute_chunk(i)
        for step in range(1, NX):
            pl.when(i == step)(lambda step=step: send_chunk(step, 0))
        return carry

    lax.fori_loop(1, NX, later, 0)

    own_copy().wait()
    for i in range(NX):

        def wait_in(j, carry):
            remote(i, j).wait_recv()
            return carry

        lax.fori_loop(1 if i == 0 else 0, NY, wait_in, 0)
        for view in range(2):
            clear = jnp.ones((BE, 128), jnp.float32)
            tints = [jnp.zeros((BE, 128), jnp.float32) for _ in range(3)]
            for rank in range(NY):
                source = jnp.bitwise_xor(rank, masks[view] & (NY - 1))
                j = (y - source) & (NY - 1)
                for ch in range(3):
                    tints[ch] = tints[ch] + clear * decode(recv[i][j, view, ch])
                clear = clear * (1.0 - decode(recv[i][j, view, 3]))
            for ch in range(3):
                group[i, view, ch] = tints[ch]
            group[i, view, 3] = clear

    for view in range(2):
        clear = jnp.ones((BE, 128), jnp.float32)
        tints = [jnp.zeros((BE, 128), jnp.float32) for _ in range(3)]
        for rank in range(NX):
            source = jnp.bitwise_xor(rank, masks[view] // NY)
            i = (x - source) & (NX - 1)
            for ch in range(3):
                tints[ch] = tints[ch] + clear * group[i, view, ch]
            clear = clear * group[i, view, 3]
        for ch, value in enumerate(tints + [1.0 - clear]):
            for h in range(2):
                out[view, ch, :, h * 128:(h + 1) * 128] = swap_rows_and_groups(value[h * 8:(h + 1) * 8, :])

    for i in range(NX):

        def wait_out(j, carry):
            remote(i, j).wait_send()
            return carry

        lax.fori_loop(1 if i == 0 else 0, NY, wait_out, 0)


def shards(bricks, cost, order, color_gain, color_bias, ext_gain, ext_bias):
    table = jnp.asarray(shear_table())
    smem = pl.BlockSpec(memory_space=pltpu.SMEM)
    vmem = pl.BlockSpec(memory_space=pltpu.VMEM)
    anywhere = pl.BlockSpec(memory_space=pl.ANY)
    return pl.pallas_call(
        kernel,
        out_shape=jax.ShapeDtypeStruct((2, 4, 8, 256), jnp.float32),
        in_specs=[smem] * 5 + [vmem, anywhere, anywhere],
        out_specs=vmem,
        scratch_shapes=[
            pltpu.VMEM((NX, CHUNK * BE, PX), jnp.bfloat16),
            pltpu.VMEM((2, BE, PX, PX), jnp.bfloat16),
            pltpu.VMEM((BE, CHUNK, PX), jnp.bfloat16),
            pltpu.VMEM((2, BE, CHUNK, PX), jnp.float32),
            pltpu.VMEM((NB, 128), jnp.float32),
            pltpu.VMEM((NX * NY, 2, 4, BE, 128), jnp.int16),
            *[pltpu.VMEM((NY, 2, 4, BE, 128), jnp.int16) for _ in range(NX)],
            pltpu.VMEM((NX, 2, 4, BE, 128), jnp.float32),
            pltpu.SemaphoreType.DMA((NX,)),
            pltpu.SemaphoreType.DMA((2,)),
            pltpu.SemaphoreType.DMA((NX * NY,)),
            pltpu.SemaphoreType.DMA((NX * NY,)),
            pltpu.SemaphoreType.DMA,
        ],
        compiler_params=pltpu.CompilerParams(
            collective_id=0, has_side_effects=True, vmem_limit_bytes=40 * 2**20
        ),
    )(order, color_gain, color_bias, ext_gain, ext_bias, cost, bricks.reshape(NB * BE, PX), table)


def solution(mesh):
    in_specs = (P("depth", "image", None, None), P("depth", "image"), P(), P(), P(), P(), P())
    out_specs = P(None, None, "depth", "image")
    return jax.shard_map(shards, mesh=mesh, in_specs=in_specs, out_specs=out_specs, check_vma=False)
```

```python
import jax
import jax.numpy as jnp
import numpy as np
import ml_dtypes
from jax import lax
from jax.experimental import pallas as pl
from jax.experimental.pallas import tpu as pltpu
from jax.sharding import PartitionSpec as P

BE = 16
PX = BE * BE
NB = 256
NX = 4
NY = 8
CHUNK = NB // NX
SHEAR = (0.45, -0.3)
LOG2E = 1.4426950408889634
TOP = 65535.0
MESH = pl.DeviceIdType.MESH


def shear_table():
    cells = np.arange(PX)
    rows, cols = cells // BE, cells % BE
    out = np.zeros((2, BE, PX, PX), np.float32)
    for view in range(2):
        k = np.arange(BE, dtype=np.float32)[:, None]
        position = np.arange(BE, dtype=np.float32)[None, :] + np.float32(SHEAR[view]) * (
            k - np.float32((BE - 1) / 2.0)
        )
        anchor = np.floor(position)
        fraction = (position - anchor).astype(np.float32)
        low = (np.float32(1.0) - fraction).astype(ml_dtypes.bfloat16).astype(np.float32)
        high = fraction.astype(ml_dtypes.bfloat16).astype(np.float32)
        anchor = anchor.astype(np.int32)
        along = cols if view == 0 else rows
        for tap, weight in ((0, low), (1, high)):
            source = anchor[:, along] + tap
            inside = (source >= 0) & (source < BE)
            for s in range(BE):
                index = (rows * BE + source[s]) if view == 0 else (source[s] * BE + cols)
                ok = inside[s]
                out[view, s, index[ok], cells[ok]] += weight[s, along][ok]
    return out.astype(ml_dtypes.bfloat16)


def encode(value):
    root = jnp.exp2(0.25 * jnp.log2(jnp.maximum(value, 1e-30)))
    code = jnp.minimum(root * TOP + 0.5, TOP).astype(jnp.int32) - 32768
    return code.astype(jnp.int16)


def decode(code):
    root = (code.astype(jnp.float32) + 32768.0) * (1.0 / TOP)
    square = root * root
    return square * square


def swap_rows_and_groups(block):
    row = lax.broadcasted_iota(jnp.int32, (8, 128), 0)
    group = lax.broadcasted_iota(jnp.int32, (8, 128), 1) // 16
    for bit in (1, 2, 4):
        row_bit = (row & bit) != 0
        group_bit = (group & bit) != 0
        from_below = pltpu.roll(pltpu.roll(block, 8 - bit, 0), 16 * bit, 1)
        from_above = pltpu.roll(pltpu.roll(block, bit, 0), 128 - 16 * bit, 1)
        moved = jnp.where(row_bit, from_above, from_below)
        block = jnp.where(row_bit == group_bit, block, moved)
    return block


def kernel(
    order_hbm, color_gain_hbm, color_bias_hbm, ext_gain_hbm, ext_bias_hbm, cost_hbm, bricks, table_hbm, out,
    order, color_gain, color_bias, ext_gain, ext_bias, cost, raw, table, sliced, samples, levels, slab, other, pair_out,
    pair_in0, pair_in1, pair_in2, pair_in3, group,
    small_sem, raw_sem, table_sem, slab_send_sem, slab_recv_sem, pair_send_sem, pair_recv_sem, own_sem,
):
    me = lax.axis_index("depth")
    x, y = me // NY, me % NY

    def chunk_copy(i):
        c = lax.rem(x + i + 1, NX)
        rows = pl.ds(pl.multiple_of(c * CHUNK * BE, CHUNK * BE), CHUNK * BE)
        return pltpu.make_async_copy(bricks.at[rows], raw.at[i], raw_sem.at[i])

    def table_copy(view):
        return pltpu.make_async_copy(table_hbm.at[view], table.at[view], table_sem.at[view])

    small = [
        pltpu.make_async_copy(source, target, small_sem.at[n])
        for n, (source, target) in enumerate((
            (cost_hbm, cost), (order_hbm, order), (ext_gain_hbm, ext_gain), (ext_bias_hbm, ext_bias),
            (color_gain_hbm, color_gain), (color_bias_hbm, color_bias),
        ))
    ]
    for copy in small:
        copy.start()
    chunk_copy(0).start()
    table_copy(0).start()
    table_copy(1).start()
    for i in range(1, NX):
        chunk_copy(i).start()

    odd = lax.rem(y, 2)
    way = 2 * odd - 1
    partner = x * NY + y - way

    def peer(i, t):
        return lax.rem(x + i, NX) * NY + lax.rem(y + way * t + NY, NY)

    barrier = pltpu.get_barrier_semaphore()

    def greet(t, carry):
        pl.semaphore_signal(barrier, inc=1, device_id={"depth": lax.rem(me + t, NX * NY)}, device_id_type=MESH)
        return carry

    lax.fori_loop(1, NX * NY, greet, 0)

    for copy in small:
        copy.wait()

    r = lax.broadcasted_iota(jnp.int32, (NB, NB), 0)
    q = lax.broadcasted_iota(jnp.int32, (NB, NB), 1)
    diagonal = jnp.where(r == q, (cost[...] * 4).astype(jnp.float32), 0.0).astype(jnp.bfloat16)
    levels[...] = jnp.dot(diagonal, jnp.ones((NB, 128), jnp.bfloat16), preferred_element_type=jnp.float32)
    regroup = jnp.where(q == (r % BE) * BE + r // BE, 1.0, 0.0).astype(jnp.bfloat16)

    masks = [order[v, 0] for v in range(2)]
    turned = [jnp.where(order[v, 0] > order[v, 31], 15, 0) for v in range(2)]
    gain = ext_gain[0] * LOG2E
    bias = ext_bias[0] * LOG2E + float(np.log2(LOG2E))
    half_gain = [color_gain[c] * 0.5 for c in range(3)]
    half_bias = [color_bias[c] * 0.5 for c in range(3)]

    pair_in = (pair_in0, pair_in1, pair_in2, pair_in3)

    def to_partner(n):
        return pltpu.make_async_remote_copy(
            src_ref=slab.at[n, pl.ds(4, 4)], dst_ref=other.at[n],
            send_sem=slab_send_sem.at[n], recv_sem=slab_recv_sem.at[n],
            device_id={"depth": partner}, device_id_type=MESH,
        )

    def to_owner(n, t):
        return pltpu.make_async_remote_copy(
            src_ref=pair_out.at[n, t], dst_ref=pair_in[n].at[t],
            send_sem=pair_send_sem.at[n * 4 + t], recv_sem=pair_recv_sem.at[n * 4 + t],
            device_id={"depth": peer(n + 1, t)}, device_id_type=MESH,
        )

    def own_copy():
        return pltpu.make_async_copy(pair_out.at[NX - 1, 0], pair_in3.at[0], own_sem)

    def compute_chunk(i):
        chunk_copy(i).wait()
        for g in range(CHUNK // BE):
            lined = jnp.dot(
                regroup, raw[i, g * PX:(g + 1) * PX, :], preferred_element_type=jnp.float32
            ).astype(jnp.bfloat16)
            for k in range(BE):
                sliced[k, g * BE:(g + 1) * BE, :] = lined[k * BE:(k + 1) * BE, :]

        for view in range(2):
            if isinstance(i, int):
                table_copy(view).wait()

            def resample(k, carry):
                samples[view, k] = jnp.dot(
                    sliced[k], table[view, k], preferred_element_type=jnp.float32
                )
                return carry

            lax.fori_loop(0, BE, resample, 0, unroll=4)

        c = lax.rem(x + i + 1, NX)
        for view in range(2):

            def shade(g, carry):
                rows = pl.ds(pl.multiple_of(g * BE, BE), BE)
                level = levels[pl.ds(pl.multiple_of(c * CHUNK + g * BE, BE), BE), :]
                level = jnp.concatenate([level, level], axis=1)
                depth = jnp.zeros((BE, PX), jnp.float32)
                clear = jnp.ones((BE, PX), jnp.float32)
                tints = [jnp.zeros((BE, PX), jnp.float32) for _ in range(3)]
                for k in range(BE):
                    kk = jnp.bitwise_xor(k, turned[view])
                    s = samples[view, kk, rows, :]
                    b = jnp.where(kk.astype(jnp.float32) < level, bias, -1e9)
                    depth = depth - jnp.exp2(s * gain + b)
                    after = jnp.exp2(depth)
                    weight = clear - after
                    clear = after
                    for ch in range(3):
                        tints[ch] = tints[ch] + weight * jnp.tanh(s * half_gain[ch] + half_bias[ch])
                opaque = 1.0 - clear
                values = [0.5 * (opaque + t) for t in tints] + [opaque]
                for ch in range(4):
                    code = encode(values[ch])
                    for h in range(2):
                        u = lax.rem(way * (2 * g + h - y) + NY, NY)
                        slab[i, u, view, ch] = code[:, h * 128:(h + 1) * 128]
                return carry

            lax.fori_loop(0, CHUNK // BE, shade, 0)

    def composite_pair(n):
        to_partner(n).wait_recv()

        def one(t, carry):
            for view in range(2):
                first = (jnp.bitwise_xor(y, masks[view]) & 1) == 0
                mine = [decode(slab[n, t, view, ch]) for ch in range(4)]
                theirs = [decode(other[n, 3 - t, view, ch]) for ch in range(4)]
                keep_mine = jnp.where(first, 1.0, 1.0 - theirs[3])
                keep_theirs = jnp.where(first, 1.0 - mine[3], 1.0)
                for ch in range(4):
                    pair_out[n, t, view, ch] = encode(keep_mine * mine[ch] + keep_theirs * theirs[ch])
            return carry

        lax.fori_loop(0, 4, one, 0)

    def send_pairs(n):
        def go(t, carry):
            to_owner(n, t).start()
            return carry

        if n == NX - 1:
            own_copy().start()
        lax.fori_loop(1 if n == NX - 1 else 0, 4, go, 0)

    compute_chunk(0)
    pl.semaphore_wait(barrier, NX * NY - 1)
    to_partner(0).start()

    def later(n, carry):
        compute_chunk(n)
        to_partner(n).start()
        composite_pair(n - 1)
        for step in range(NX - 1):
            pl.when(n - 1 == step)(lambda step=step: send_pairs(step))
        return carry

    lax.fori_loop(1, NX, later, 0)
    composite_pair(NX - 1)
    send_pairs(NX - 1)

    for n in range(NX):
        first = 0
        if n == NX - 1:
            own_copy().wait()
            first = 1

        def wait_in(t, carry):
            to_owner(n, t).wait_recv()
            return carry

        lax.fori_loop(first, 4, wait_in, 0)
        for view in range(2):
            clear = jnp.ones((BE, 128), jnp.float32)
            total = [jnp.zeros((BE, 128), jnp.float32) for _ in range(4)]
            for rank in range(4):
                pair = jnp.bitwise_xor(rank, (masks[view] // 2) & 3)
                delta = (way * (pair - y // 2)) & 3
                t = jnp.bitwise_xor(delta, delta // 2)
                for ch in range(4):
                    total[ch] = total[ch] + clear * decode(pair_in[n][t, view, ch])
                clear = 1.0 - total[3]
            for ch in range(4):
                group[n, view, ch] = total[ch]

    for view in range(2):
        clear = jnp.ones((BE, 128), jnp.float32)
        total = [jnp.zeros((BE, 128), jnp.float32) for _ in range(4)]
        for rank in range(NX):
            source = jnp.bitwise_xor(rank, masks[view] // NY)
            n = (x - source - 1) & (NX - 1)
            for ch in range(4):
                total[ch] = total[ch] + clear * group[n, view, ch]
            clear = 1.0 - total[3]
        for ch in range(4):
            for h in range(2):
                out[view, ch, :, h * 128:(h + 1) * 128] = swap_rows_and_groups(total[ch][h * 8:(h + 1) * 8, :])

    for n in range(NX):
        to_partner(n).wait_send()

        def wait_out(t, carry):
            to_owner(n, t).wait_send()
            return carry

        lax.fori_loop(1 if n == NX - 1 else 0, 4, wait_out, 0)


def shards(bricks, cost, order, color_gain, color_bias, ext_gain, ext_bias):
    table = jnp.asarray(shear_table())
    vmem = pl.BlockSpec(memory_space=pltpu.VMEM)
    anywhere = pl.BlockSpec(memory_space=pltpu.HBM)
    return pl.pallas_call(
        kernel,
        out_shape=jax.ShapeDtypeStruct((2, 4, 8, 256), jnp.float32),
        in_specs=[anywhere] * 8,
        out_specs=vmem,
        scratch_shapes=[
            pltpu.SMEM((2, 32), jnp.int32),
            pltpu.SMEM((3,), jnp.float32),
            pltpu.SMEM((3,), jnp.float32),
            pltpu.SMEM((1,), jnp.float32),
            pltpu.SMEM((1,), jnp.float32),
            pltpu.VMEM((1, NB), jnp.int32),
            pltpu.VMEM((NX, CHUNK * BE, PX), jnp.bfloat16),
            pltpu.VMEM((2, BE, PX, PX), jnp.bfloat16),
            pltpu.VMEM((BE, CHUNK, PX), jnp.bfloat16),
            pltpu.VMEM((2, BE, CHUNK, PX), jnp.float32),
            pltpu.VMEM((NB, 128), jnp.float32),
            pltpu.VMEM((NX, 8, 2, 4, BE, 128), jnp.int16),
            pltpu.VMEM((NX, 4, 2, 4, BE, 128), jnp.int16),
            pltpu.VMEM((NX, 4, 2, 4, BE, 128), jnp.int16),
            *[pltpu.VMEM((4, 2, 4, BE, 128), jnp.int16) for _ in range(NX)],
            pltpu.VMEM((NX, 2, 4, BE, 128), jnp.float32),
            pltpu.SemaphoreType.DMA((6,)),
            pltpu.SemaphoreType.DMA((NX,)),
            pltpu.SemaphoreType.DMA((2,)),
            pltpu.SemaphoreType.DMA((NX,)),
            pltpu.SemaphoreType.DMA((NX,)),
            pltpu.SemaphoreType.DMA((NX * 4,)),
            pltpu.SemaphoreType.DMA((NX * 4,)),
            pltpu.SemaphoreType.DMA,
        ],
        compiler_params=pltpu.CompilerParams(
            collective_id=0, has_side_effects=True, vmem_limit_bytes=58 * 2**20
        ),
    )(order, color_gain, color_bias, ext_gain, ext_bias, cost, bricks.reshape(NB * BE, PX), table)


def solution(mesh):
    in_specs = (P("depth", "image", None, None), P("depth", "image"), P(), P(), P(), P(), P())
    out_specs = P(None, None, "depth", "image")
    return jax.shard_map(shards, mesh=mesh, in_specs=in_specs, out_specs=out_specs, check_vma=False)
```

```python
import jax
import jax.numpy as jnp
import numpy as np
import ml_dtypes
from jax import lax
from jax.experimental import pallas as pl
from jax.experimental.pallas import tpu as pltpu
from jax.sharding import PartitionSpec as P

BE = 16
PX = BE * BE
NB = 256
NX = 4
NY = 8
CHUNK = NB // NX
SHEAR = (0.45, -0.3)
LOG2E = 1.4426950408889634
TOP = 65535.0
MESH = pl.DeviceIdType.MESH


def shear_table():
    cells = np.arange(PX)
    rows, cols = cells // BE, cells % BE
    out = np.zeros((2, BE, PX, PX), np.float32)
    for view in range(2):
        k = np.arange(BE, dtype=np.float32)[:, None]
        position = np.arange(BE, dtype=np.float32)[None, :] + np.float32(SHEAR[view]) * (
            k - np.float32((BE - 1) / 2.0)
        )
        anchor = np.floor(position)
        fraction = (position - anchor).astype(np.float32)
        low = (np.float32(1.0) - fraction).astype(ml_dtypes.bfloat16).astype(np.float32)
        high = fraction.astype(ml_dtypes.bfloat16).astype(np.float32)
        anchor = anchor.astype(np.int32)
        along = cols if view == 0 else rows
        for tap, weight in ((0, low), (1, high)):
            source = anchor[:, along] + tap
            inside = (source >= 0) & (source < BE)
            for s in range(BE):
                index = (rows * BE + source[s]) if view == 0 else (source[s] * BE + cols)
                ok = inside[s]
                out[view, s, index[ok], cells[ok]] += weight[s, along][ok]
    return out.astype(ml_dtypes.bfloat16)


def encode(value):
    root = jnp.exp2(0.25 * jnp.log2(jnp.maximum(value, 1e-30)))
    code = jnp.minimum(root * TOP + 0.5, TOP).astype(jnp.int32) - 32768
    return code.astype(jnp.int16)


def decode(code):
    root = (code.astype(jnp.float32) + 32768.0) * (1.0 / TOP)
    square = root * root
    return square * square


def swap_rows_and_groups(block):
    row = lax.broadcasted_iota(jnp.int32, (8, 128), 0)
    group = lax.broadcasted_iota(jnp.int32, (8, 128), 1) // 16
    for bit in (1, 2, 4):
        row_bit = (row & bit) != 0
        group_bit = (group & bit) != 0
        from_below = pltpu.roll(pltpu.roll(block, 8 - bit, 0), 16 * bit, 1)
        from_above = pltpu.roll(pltpu.roll(block, bit, 0), 128 - 16 * bit, 1)
        moved = jnp.where(row_bit, from_above, from_below)
        block = jnp.where(row_bit == group_bit, block, moved)
    return block


def kernel(
    order_hbm, color_gain_hbm, color_bias_hbm, ext_gain_hbm, ext_bias_hbm, cost_hbm, bricks, table_hbm, out,
    order, color_gain, color_bias, ext_gain, ext_bias, cost, raw, table, sliced, samples, offset, slab, other, pair_out, *rest,
):
    pair_in = (rest[:NX], rest[NX:2 * NX])
    (
        group, small_sem, raw_sem, table_sem, slab_send_sem, slab_recv_sem,
        pair_send_sem, pair_recv_sem, own_sem,
    ) = rest[2 * NX:]
    me = lax.axis_index("depth")
    x, y = me // NY, me % NY

    def chunk_copy(i):
        c = lax.rem(x + i + 1, NX)
        rows = pl.ds(pl.multiple_of(c * CHUNK * BE, CHUNK * BE), CHUNK * BE)
        return pltpu.make_async_copy(bricks.at[rows], raw.at[i], raw_sem.at[i])

    def table_copy(view):
        return pltpu.make_async_copy(table_hbm.at[view], table.at[view], table_sem.at[view])

    small = [
        pltpu.make_async_copy(source, target, small_sem.at[n])
        for n, (source, target) in enumerate((
            (cost_hbm, cost), (order_hbm, order), (ext_gain_hbm, ext_gain), (ext_bias_hbm, ext_bias),
            (color_gain_hbm, color_gain), (color_bias_hbm, color_bias),
        ))
    ]
    for copy in small:
        copy.start()
    chunk_copy(0).start()
    table_copy(0).start()
    table_copy(1).start()
    for i in range(1, NX):
        chunk_copy(i).start()

    odd = lax.rem(y, 2)
    way = 2 * odd - 1
    partner = x * NY + y - way

    def peer(i, t):
        return lax.rem(x + i, NX) * NY + lax.rem(y + way * t + NY, NY)

    barrier = pltpu.get_barrier_semaphore()

    def greet(device):
        pl.semaphore_signal(barrier, inc=1, device_id={"depth": device}, device_id_type=MESH)

    greet(partner)
    for i in range(NX):
        for t, step in enumerate((0, way, -2 * way, 3 * way)):
            if i or t:
                greet(lax.rem(x + NX - i, NX) * NY + lax.rem(y + step + NY, NY))

    for copy in small:
        copy.wait()

    r = lax.broadcasted_iota(jnp.int32, (NB, NB), 0)
    q = lax.broadcasted_iota(jnp.int32, (NB, NB), 1)
    diagonal = jnp.where(r == q, (cost[...] * 4).astype(jnp.float32), 0.0).astype(jnp.bfloat16)
    level = jnp.dot(diagonal, jnp.ones((NB, 128), jnp.bfloat16), preferred_element_type=jnp.float32)
    gain = ext_gain[0] * LOG2E
    bias = ext_bias[0] * LOG2E + float(np.log2(LOG2E))
    for k in range(BE):
        offset[k] = jnp.where(k < level, bias, -1e9)
    regroup = jnp.where(q == (r % BE) * BE + r // BE, 1.0, 0.0).astype(jnp.bfloat16)

    masks = [order[v, 0] for v in range(2)]
    turned = [jnp.where(order[v, 0] > order[v, 31], 15, 0) for v in range(2)]
    half_gain = [color_gain[c] * 0.5 for c in range(3)]
    half_bias = [color_bias[c] * 0.5 for c in range(3)]

    def to_partner(view, n):
        return pltpu.make_async_remote_copy(
            src_ref=slab.at[view, n, pl.ds(4, 4)], dst_ref=other.at[view, n],
            send_sem=slab_send_sem.at[view * NX + n], recv_sem=slab_recv_sem.at[view * NX + n],
            device_id={"depth": partner}, device_id_type=MESH,
        )

    def to_owner(view, n, t):
        sem = (view * NX + n) * 4 + t
        return pltpu.make_async_remote_copy(
            src_ref=pair_out.at[view, n, t], dst_ref=pair_in[view][n].at[t],
            send_sem=pair_send_sem.at[sem], recv_sem=pair_recv_sem.at[sem],
            device_id={"depth": peer(n + 1, t)}, device_id_type=MESH,
        )

    def own_copy(view):
        return pltpu.make_async_copy(
            pair_out.at[view, NX - 1, 0], pair_in[view][NX - 1].at[0], own_sem.at[view]
        )

    def regroup_chunk(i):
        chunk_copy(i).wait()
        for g in range(CHUNK // BE):
            lined = jnp.dot(
                regroup, raw[i, g * PX:(g + 1) * PX, :], preferred_element_type=jnp.float32
            ).astype(jnp.bfloat16)
            rows = pl.ds(pl.multiple_of(i * CHUNK + g * BE, BE), BE)
            for k in range(BE):
                sliced[k, rows, :] = lined[k * BE:(k + 1) * BE, :]

    def resample_rows(view, first, count):
        def resample(k, carry):
            mixed = jnp.dot(
                sliced[k, first:first + count], table[view, k], preferred_element_type=jnp.float32
            )
            for h in range(2):
                samples[view, k, h, first:first + count] = mixed[:, h * 128:(h + 1) * 128]
            return carry

        lax.fori_loop(0, BE, resample, 0, unroll=4)

    def shade_part(view, n, part):
        c = lax.rem(x + n + 1, NX)

        def shade(pair, carry):
            places = []
            for e in range(2):
                u = part * 4 + pair * 2 + e
                row = lax.rem(y + way * u + NY, NY)
                g, h = row // 2, lax.rem(row, 2)
                places.append((
                    u, h, pl.ds(pl.multiple_of(n * CHUNK + g * BE, BE), BE),
                    pl.ds(pl.multiple_of(c * CHUNK + g * BE, BE), BE),
                ))
            depth = jnp.zeros((2 * BE, 128), jnp.float32)
            clear = jnp.ones((2 * BE, 128), jnp.float32)
            tints = [jnp.zeros((2 * BE, 128), jnp.float32) for _ in range(3)]
            for k in range(BE):
                kk = jnp.bitwise_xor(k, turned[view])
                s = jnp.concatenate([samples[view, kk, h, rows, :] for _, h, rows, _ in places], axis=0)
                b = jnp.concatenate([offset[kk, rows, :] for _, _, _, rows in places], axis=0)
                depth = depth - jnp.exp2(s * gain + b)
                after = jnp.exp2(depth)
                weight = clear - after
                clear = after
                for ch in range(3):
                    tints[ch] = tints[ch] + weight * jnp.tanh(s * half_gain[ch] + half_bias[ch])
            opaque = 1.0 - clear
            values = [0.5 * (opaque + t) for t in tints] + [opaque]
            for ch in range(4):
                code = encode(values[ch])
                for e in range(2):
                    slab[view, n, places[e][0], ch] = code[e * BE:(e + 1) * BE]
            return carry

        lax.fori_loop(0, 2, shade, 0)

    def send_slab(view, n):
        shade_part(view, n, 1)
        to_partner(view, n).start()

    def composite_pair(view, n):
        first = (jnp.bitwise_xor(y, masks[view]) & 1) == 0
        to_partner(view, n).wait_recv()

        def one(t, carry):
            mine = [decode(slab[view, n, t, ch]) for ch in range(4)]
            theirs = [decode(other[view, n, 3 - t, ch]) for ch in range(4)]
            keep_mine = jnp.where(first, 1.0, 1.0 - theirs[3])
            keep_theirs = jnp.where(first, 1.0 - mine[3], 1.0)
            for ch in range(4):
                pair_out[view, n, t, ch] = encode(keep_mine * mine[ch] + keep_theirs * theirs[ch])
            return carry

        lax.fori_loop(0, 4, one, 0)

    def send_pairs(view, n):
        def go(t, carry):
            to_owner(view, n, t).start()
            return carry

        if n == NX - 1:
            own_copy(view).start()
        lax.fori_loop(1 if n == NX - 1 else 0, 4, go, 0)

    def finish_column(view, n):
        shade_part(view, n, 0)
        composite_pair(view, n)
        for step in range(NX):
            pl.when(n == step)(lambda step=step: send_pairs(view, step))

    def loop(start, body):
        def step(n, carry):
            body(n)
            return carry

        lax.fori_loop(start, NX, step, 0)

    regroup_chunk(0)
    table_copy(0).wait()
    resample_rows(0, 0, CHUNK)
    shade_part(0, 0, 1)
    pl.semaphore_wait(barrier, 4 * NX)
    to_partner(0, 0).start()
    loop(1, regroup_chunk)
    resample_rows(0, CHUNK, NB - CHUNK)
    loop(1, lambda n: send_slab(0, n))
    table_copy(1).wait()
    resample_rows(1, 0, NB)

    def both(n):
        send_slab(1, n)
        finish_column(0, n)

    loop(0, both)
    loop(0, lambda n: finish_column(1, n))

    for view in range(2):
        for n in range(NX):
            first = 0
            if n == NX - 1:
                own_copy(view).wait()
                first = 1

            def wait_in(t, carry):
                to_owner(view, n, t).wait_recv()
                return carry

            lax.fori_loop(first, 4, wait_in, 0)
            clear = jnp.ones((BE, 128), jnp.float32)
            total = [jnp.zeros((BE, 128), jnp.float32) for _ in range(4)]
            for rank in range(4):
                pair = jnp.bitwise_xor(rank, (masks[view] // 2) & 3)
                delta = (way * (pair - y // 2)) & 3
                t = jnp.bitwise_xor(delta, delta // 2)
                for ch in range(4):
                    total[ch] = total[ch] + clear * decode(pair_in[view][n][t, ch])
                clear = 1.0 - total[3]
            for ch in range(4):
                group[view, n, ch] = total[ch]

        clear = jnp.ones((BE, 128), jnp.float32)
        total = [jnp.zeros((BE, 128), jnp.float32) for _ in range(4)]
        for rank in range(NX):
            source = jnp.bitwise_xor(rank, masks[view] // NY)
            n = (x - source - 1) & (NX - 1)
            for ch in range(4):
                total[ch] = total[ch] + clear * group[view, n, ch]
            clear = 1.0 - total[3]
        for ch in range(4):
            for h in range(2):
                out[view, ch, :, h * 128:(h + 1) * 128] = swap_rows_and_groups(total[ch][h * 8:(h + 1) * 8, :])

    for view in range(2):
        for n in range(NX):
            to_partner(view, n).wait_send()

            def wait_out(t, carry):
                to_owner(view, n, t).wait_send()
                return carry

            lax.fori_loop(1 if n == NX - 1 else 0, 4, wait_out, 0)


def shards(bricks, cost, order, color_gain, color_bias, ext_gain, ext_bias):
    table = jnp.asarray(shear_table())
    vmem = pl.BlockSpec(memory_space=pltpu.VMEM)
    anywhere = pl.BlockSpec(memory_space=pltpu.HBM)
    return pl.pallas_call(
        kernel,
        out_shape=jax.ShapeDtypeStruct((2, 4, 8, 256), jnp.float32),
        in_specs=[anywhere] * 8,
        out_specs=vmem,
        scratch_shapes=[
            pltpu.SMEM((2, 32), jnp.int32),
            pltpu.SMEM((3,), jnp.float32),
            pltpu.SMEM((3,), jnp.float32),
            pltpu.SMEM((1,), jnp.float32),
            pltpu.SMEM((1,), jnp.float32),
            pltpu.VMEM((1, NB), jnp.int32),
            pltpu.VMEM((NX, CHUNK * BE, PX), jnp.bfloat16),
            pltpu.VMEM((2, BE, PX, PX), jnp.bfloat16),
            pltpu.VMEM((BE, NB, PX), jnp.bfloat16),
            pltpu.VMEM((2, BE, 2, NB, 128), jnp.float32),
            pltpu.VMEM((BE, NB, 128), jnp.float32),
            pltpu.VMEM((2, NX, 8, 4, BE, 128), jnp.int16),
            pltpu.VMEM((2, NX, 4, 4, BE, 128), jnp.int16),
            pltpu.VMEM((2, NX, 4, 4, BE, 128), jnp.int16),
            *[pltpu.VMEM((4, 4, BE, 128), jnp.int16) for _ in range(2 * NX)],
            pltpu.VMEM((2, NX, 4, BE, 128), jnp.float32),
            pltpu.SemaphoreType.DMA((6,)),
            pltpu.SemaphoreType.DMA((NX,)),
            pltpu.SemaphoreType.DMA((2,)),
            pltpu.SemaphoreType.DMA((NX * 2,)),
            pltpu.SemaphoreType.DMA((NX * 2,)),
            pltpu.SemaphoreType.DMA((2 * NX * 4,)),
            pltpu.SemaphoreType.DMA((2 * NX * 4,)),
            pltpu.SemaphoreType.DMA((2,)),
        ],
        compiler_params=pltpu.CompilerParams(
            collective_id=0, has_side_effects=True, vmem_limit_bytes=58 * 2**20
        ),
    )(order, color_gain, color_bias, ext_gain, ext_bias, cost, bricks.reshape(NB * BE, PX), table)


def solution(mesh):
    in_specs = (P("depth", "image", None, None), P("depth", "image"), P(), P(), P(), P(), P())
    out_specs = P(None, None, "depth", "image")
    return jax.shard_map(shards, mesh=mesh, in_specs=in_specs, out_specs=out_specs, check_vma=False)
```

```python
import jax
import jax.numpy as jnp
import numpy as np
import ml_dtypes
from jax import lax
from jax.experimental import pallas as pl
from jax.experimental.pallas import tpu as pltpu
from jax.sharding import PartitionSpec as P

BE = 16
PX = BE * BE
NB = 256
NX = 4
NY = 8
CHUNK = NB // NX
SHEAR = (0.45, -0.3)
LOG2E = 1.4426950408889634
TOP = 65535.0
MESH = pl.DeviceIdType.MESH


def shear_table():
    cells = np.arange(PX)
    rows, cols = cells // BE, cells % BE
    out = np.zeros((2, BE, PX, PX), np.float32)
    for view in range(2):
        k = np.arange(BE, dtype=np.float32)[:, None]
        position = np.arange(BE, dtype=np.float32)[None, :] + np.float32(SHEAR[view]) * (
            k - np.float32((BE - 1) / 2.0)
        )
        anchor = np.floor(position)
        fraction = (position - anchor).astype(np.float32)
        low = (np.float32(1.0) - fraction).astype(ml_dtypes.bfloat16).astype(np.float32)
        high = fraction.astype(ml_dtypes.bfloat16).astype(np.float32)
        anchor = anchor.astype(np.int32)
        along = cols if view == 0 else rows
        for tap, weight in ((0, low), (1, high)):
            source = anchor[:, along] + tap
            inside = (source >= 0) & (source < BE)
            for s in range(BE):
                index = (rows * BE + source[s]) if view == 0 else (source[s] * BE + cols)
                ok = inside[s]
                out[view, s, index[ok], cells[ok]] += weight[s, along][ok]
    return out.astype(ml_dtypes.bfloat16)


def encode(value):
    root = jnp.exp2(0.25 * jnp.log2(jnp.maximum(value, 1e-30)))
    code = jnp.minimum(root * TOP + 0.5, TOP).astype(jnp.int32) - 32768
    return code.astype(jnp.int16)


def decode(code):
    root = (code.astype(jnp.float32) + 32768.0) * (1.0 / TOP)
    square = root * root
    return square * square


def swap_rows_and_groups(block):
    row = lax.broadcasted_iota(jnp.int32, (8, 128), 0)
    group = lax.broadcasted_iota(jnp.int32, (8, 128), 1) // 16
    for bit in (1, 2, 4):
        row_bit = (row & bit) != 0
        group_bit = (group & bit) != 0
        from_below = pltpu.roll(pltpu.roll(block, 8 - bit, 0), 16 * bit, 1)
        from_above = pltpu.roll(pltpu.roll(block, bit, 0), 128 - 16 * bit, 1)
        moved = jnp.where(row_bit, from_above, from_below)
        block = jnp.where(row_bit == group_bit, block, moved)
    return block


def kernel(
    order_hbm, color_gain_hbm, color_bias_hbm, ext_gain_hbm, ext_bias_hbm, cost_hbm, bricks, cell_hbm, table_hbm, out,
    order, color_gain, color_bias, ext_gain, ext_bias, cost, raw, cell, table, sliced, samples, offset, slab, other, pair_out, *rest,
):
    pair_in = (rest[:NX], rest[NX:2 * NX])
    (
        group, small_sem, raw_sem, table_sem, slab_send_sem, slab_recv_sem,
        pair_send_sem, pair_recv_sem, own_sem,
    ) = rest[2 * NX:]
    me = lax.axis_index("depth")
    x, y = me // NY, me % NY

    def chunk_copy(i):
        c = lax.rem(x + i + 1, NX)
        rows = pl.ds(pl.multiple_of(c * CHUNK * BE, CHUNK * BE), CHUNK * BE)
        return pltpu.make_async_copy(bricks.at[rows], raw.at[i], raw_sem.at[i])

    cell_copy = pltpu.make_async_copy(cell_hbm, cell, table_sem.at[0])
    table_copy = pltpu.make_async_copy(table_hbm, table.at[1], table_sem.at[1])

    small = [
        pltpu.make_async_copy(source, target, small_sem.at[n])
        for n, (source, target) in enumerate((
            (cost_hbm, cost), (order_hbm, order), (ext_gain_hbm, ext_gain), (ext_bias_hbm, ext_bias),
            (color_gain_hbm, color_gain), (color_bias_hbm, color_bias),
        ))
    ]
    for copy in small:
        copy.start()
    cell_copy.start()
    for i in range(NX):
        chunk_copy(i).start()
    table_copy.start()

    odd = lax.rem(y, 2)
    way = 2 * odd - 1
    partner = x * NY + y - way

    def peer(i, t):
        return lax.rem(x + i, NX) * NY + lax.rem(y + way * t + NY, NY)

    barrier = pltpu.get_barrier_semaphore()

    def greet(device):
        pl.semaphore_signal(barrier, inc=1, device_id={"depth": device}, device_id_type=MESH)

    greet(partner)
    for i in range(NX):
        for t, step in enumerate((0, way, -2 * way, 3 * way)):
            if i or t:
                greet(lax.rem(x + NX - i, NX) * NY + lax.rem(y + step + NY, NY))

    for copy in small:
        copy.wait()

    r = lax.broadcasted_iota(jnp.int32, (NB, NB), 0)
    q = lax.broadcasted_iota(jnp.int32, (NB, NB), 1)
    diagonal = jnp.where(r == q, (cost[...] * 4).astype(jnp.float32), 0.0).astype(jnp.bfloat16)
    level = jnp.dot(diagonal, jnp.ones((NB, 128), jnp.bfloat16), preferred_element_type=jnp.float32)
    gain = ext_gain[0] * LOG2E
    bias = ext_bias[0] * LOG2E + float(np.log2(LOG2E))
    for k in range(BE):
        offset[k] = jnp.where(k < level, bias, -1e9)
    regroup = jnp.where(q == (r % BE) * BE + r // BE, 1.0, 0.0).astype(jnp.bfloat16)

    masks = [order[v, 0] for v in range(2)]
    turned = [jnp.where(order[v, 0] > order[v, 31], 15, 0) for v in range(2)]
    half_gain = [color_gain[c] * 0.5 for c in range(3)]
    half_bias = [color_bias[c] * 0.5 for c in range(3)]

    def to_partner(view, n):
        return pltpu.make_async_remote_copy(
            src_ref=slab.at[view, n, pl.ds(4, 4)], dst_ref=other.at[view, n],
            send_sem=slab_send_sem.at[view * NX + n], recv_sem=slab_recv_sem.at[view * NX + n],
            device_id={"depth": partner}, device_id_type=MESH,
        )

    def to_owner(view, n, t):
        sem = (view * NX + n) * 4 + t
        return pltpu.make_async_remote_copy(
            src_ref=pair_out.at[view, n, t], dst_ref=pair_in[view][n].at[t],
            send_sem=pair_send_sem.at[sem], recv_sem=pair_recv_sem.at[sem],
            device_id={"depth": peer(n + 1, t)}, device_id_type=MESH,
        )

    def own_copy(view):
        return pltpu.make_async_copy(
            pair_out.at[view, NX - 1, 0], pair_in[view][NX - 1].at[0], own_sem.at[view]
        )

    def regroup_chunk(i):
        chunk_copy(i).wait()
        for g in range(CHUNK // BE):
            lined = jnp.dot(
                regroup, raw[i, g * PX:(g + 1) * PX, :], preferred_element_type=jnp.float32
            ).astype(jnp.bfloat16)
            rows = pl.ds(pl.multiple_of(i * CHUNK + g * BE, BE), BE)
            for k in range(BE):
                sliced[k, rows, :] = lined[k * BE:(k + 1) * BE, :]

    def resample_rows(view, first, count):
        def resample(k, carry):
            mixed = jnp.dot(
                sliced[k, first:first + count], table[view, k], preferred_element_type=jnp.float32
            )
            for h in range(2):
                samples[view, k, h, first:first + count] = mixed[:, h * 128:(h + 1) * 128]
            return carry

        lax.fori_loop(0, BE, resample, 0, unroll=16)

    def shade_part(view, n, part):
        c = lax.rem(x + n + 1, NX)

        def shade(pair, carry):
            places = []
            for e in range(2):
                u = part * 4 + pair * 2 + e
                row = lax.rem(y + way * u + NY, NY)
                g, h = row // 2, lax.rem(row, 2)
                places.append((
                    u, h, pl.ds(pl.multiple_of(n * CHUNK + g * BE, BE), BE),
                    pl.ds(pl.multiple_of(c * CHUNK + g * BE, BE), BE),
                ))
            depth = jnp.zeros((2 * BE, 128), jnp.float32)
            clear = jnp.ones((2 * BE, 128), jnp.float32)
            tints = [jnp.zeros((2 * BE, 128), jnp.float32) for _ in range(3)]
            for k in range(BE):
                kk = jnp.bitwise_xor(k, turned[view])
                s = jnp.concatenate([samples[view, kk, h, rows, :] for _, h, rows, _ in places], axis=0)
                b = jnp.concatenate([offset[kk, rows, :] for _, _, _, rows in places], axis=0)
                depth = depth - jnp.exp2(s * gain + b)
                after = jnp.exp2(depth)
                weight = clear - after
                clear = after
                for ch in range(3):
                    tints[ch] = tints[ch] + weight * jnp.tanh(s * half_gain[ch] + half_bias[ch])
            opaque = 1.0 - clear
            values = [0.5 * (opaque + t) for t in tints] + [opaque]
            for ch in range(4):
                code = encode(values[ch])
                for e in range(2):
                    slab[view, n, places[e][0], ch] = code[e * BE:(e + 1) * BE]
            return carry

        lax.fori_loop(0, 2, shade, 0)

    def send_slab(view, n):
        shade_part(view, n, 1)
        to_partner(view, n).start()

    def composite_pair(view, n):
        first = (jnp.bitwise_xor(y, masks[view]) & 1) == 0
        to_partner(view, n).wait_recv()

        def one(t, carry):
            mine = [decode(slab[view, n, t, ch]) for ch in range(4)]
            theirs = [decode(other[view, n, 3 - t, ch]) for ch in range(4)]
            keep_mine = jnp.where(first, 1.0, 1.0 - theirs[3])
            keep_theirs = jnp.where(first, 1.0 - mine[3], 1.0)
            for ch in range(4):
                pair_out[view, n, t, ch] = encode(keep_mine * mine[ch] + keep_theirs * theirs[ch])
            return carry

        lax.fori_loop(0, 4, one, 0)

    def send_pairs(view, n):
        def go(t, carry):
            to_owner(view, n, t).start()
            return carry

        if n == NX - 1:
            own_copy(view).start()
        lax.fori_loop(1 if n == NX - 1 else 0, 4, go, 0)

    def finish_column(view, n):
        shade_part(view, n, 0)
        composite_pair(view, n)
        for step in range(NX):
            pl.when(n == step)(lambda step=step: send_pairs(view, step))

    def loop(start, body):
        def step(n, carry):
            body(n)
            return carry

        lax.fori_loop(start, NX, step, 0)

    group_of = lax.broadcasted_iota(jnp.int32, (BE, 128), 1) // BE
    keep = [jnp.where(group_of == i, 1.0, 0.0).astype(jnp.bfloat16) for i in range(8)]
    nothing = jnp.zeros((BE, 128), jnp.bfloat16)
    cell_copy.wait()

    def spread(k, carry):
        for i in range(BE):
            for j in range(2):
                table[0, k, i * BE:(i + 1) * BE, j * 128:(j + 1) * 128] = (
                    cell[k] * keep[i % 8] if i // 8 == j else nothing
                )
        return carry

    lax.fori_loop(0, BE, spread, 0)
    regroup_chunk(0)
    resample_rows(0, 0, CHUNK)
    shade_part(0, 0, 1)
    pl.semaphore_wait(barrier, 4 * NX)
    to_partner(0, 0).start()
    loop(1, regroup_chunk)
    resample_rows(0, CHUNK, NB - CHUNK)
    loop(1, lambda n: send_slab(0, n))
    table_copy.wait()
    resample_rows(1, 0, NB)

    def both(n):
        send_slab(1, n)
        finish_column(0, n)

    loop(0, both)
    loop(0, lambda n: finish_column(1, n))

    for view in range(2):
        for n in range(NX):
            first = 0
            if n == NX - 1:
                own_copy(view).wait()
                first = 1

            def wait_in(t, carry):
                to_owner(view, n, t).wait_recv()
                return carry

            lax.fori_loop(first, 4, wait_in, 0)
            clear = jnp.ones((BE, 128), jnp.float32)
            total = [jnp.zeros((BE, 128), jnp.float32) for _ in range(4)]
            for rank in range(4):
                pair = jnp.bitwise_xor(rank, (masks[view] // 2) & 3)
                delta = (way * (pair - y // 2)) & 3
                t = jnp.bitwise_xor(delta, delta // 2)
                for ch in range(4):
                    total[ch] = total[ch] + clear * decode(pair_in[view][n][t, ch])
                clear = 1.0 - total[3]
            for ch in range(4):
                group[view, n, ch] = total[ch]

        clear = jnp.ones((BE, 128), jnp.float32)
        total = [jnp.zeros((BE, 128), jnp.float32) for _ in range(4)]
        for rank in range(NX):
            source = jnp.bitwise_xor(rank, masks[view] // NY)
            n = (x - source - 1) & (NX - 1)
            for ch in range(4):
                total[ch] = total[ch] + clear * group[view, n, ch]
            clear = 1.0 - total[3]
        for ch in range(4):
            for h in range(2):
                out[view, ch, :, h * 128:(h + 1) * 128] = swap_rows_and_groups(total[ch][h * 8:(h + 1) * 8, :])

    for view in range(2):
        for n in range(NX):
            to_partner(view, n).wait_send()

            def wait_out(t, carry):
                to_owner(view, n, t).wait_send()
                return carry

            lax.fori_loop(1 if n == NX - 1 else 0, 4, wait_out, 0)


def shards(bricks, cost, order, color_gain, color_bias, ext_gain, ext_bias):
    tables = shear_table()
    cell = jnp.asarray(np.tile(tables[0, :, :BE, :BE], (1, 1, 8)))
    table = jnp.asarray(tables[1])
    vmem = pl.BlockSpec(memory_space=pltpu.VMEM)

    def hbm(array):
        return pltpu.with_memory_space_constraint(array, pltpu.HBM)

    anywhere = pl.BlockSpec(memory_space=pltpu.HBM)
    return pl.pallas_call(
        kernel,
        out_shape=jax.ShapeDtypeStruct((2, 4, 8, 256), jnp.float32),
        in_specs=[anywhere] * 9,
        out_specs=vmem,
        scratch_shapes=[
            pltpu.SMEM((2, 32), jnp.int32),
            pltpu.SMEM((3,), jnp.float32),
            pltpu.SMEM((3,), jnp.float32),
            pltpu.SMEM((1,), jnp.float32),
            pltpu.SMEM((1,), jnp.float32),
            pltpu.VMEM((1, NB), jnp.int32),
            pltpu.VMEM((NX, CHUNK * BE, PX), jnp.bfloat16),
            pltpu.VMEM((BE, BE, 128), jnp.bfloat16),
            pltpu.VMEM((2, BE, PX, PX), jnp.bfloat16),
            pltpu.VMEM((BE, NB, PX), jnp.bfloat16),
            pltpu.VMEM((2, BE, 2, NB, 128), jnp.float32),
            pltpu.VMEM((BE, NB, 128), jnp.float32),
            pltpu.VMEM((2, NX, 8, 4, BE, 128), jnp.int16),
            pltpu.VMEM((2, NX, 4, 4, BE, 128), jnp.int16),
            pltpu.VMEM((2, NX, 4, 4, BE, 128), jnp.int16),
            *[pltpu.VMEM((4, 4, BE, 128), jnp.int16) for _ in range(2 * NX)],
            pltpu.VMEM((2, NX, 4, BE, 128), jnp.float32),
            pltpu.SemaphoreType.DMA((6,)),
            pltpu.SemaphoreType.DMA((NX,)),
            pltpu.SemaphoreType.DMA((2,)),
            pltpu.SemaphoreType.DMA((NX * 2,)),
            pltpu.SemaphoreType.DMA((NX * 2,)),
            pltpu.SemaphoreType.DMA((2 * NX * 4,)),
            pltpu.SemaphoreType.DMA((2 * NX * 4,)),
            pltpu.SemaphoreType.DMA((2,)),
        ],
        compiler_params=pltpu.CompilerParams(
            collective_id=0, has_side_effects=True, vmem_limit_bytes=48 * 2**20
        ),
    )(hbm(order), hbm(color_gain), hbm(color_bias), ext_gain, ext_bias, hbm(cost), hbm(bricks.reshape(NB * BE, PX)), hbm(cell), hbm(table))


def solution(mesh):
    in_specs = (P("depth", "image", None, None), P("depth", "image"), P(), P(), P(), P(), P())
    out_specs = P(None, None, "depth", "image")
    return jax.shard_map(shards, mesh=mesh, in_specs=in_specs, out_specs=out_specs, check_vma=False)
```

```python
import jax
import jax.numpy as jnp
import numpy as np
import ml_dtypes
from jax import lax
from jax.experimental import pallas as pl
from jax.experimental.pallas import tpu as pltpu
from jax.sharding import PartitionSpec as P

BE = 16
PX = BE * BE
NB = 256
NX = 4
NY = 8
CHUNK = NB // NX
SHEAR = (0.45, -0.3)
LOG2E = 1.4426950408889634
TOP = 65535.0
MESH = pl.DeviceIdType.MESH


def shear_table():
    cells = np.arange(PX)
    rows, cols = cells // BE, cells % BE
    out = np.zeros((2, BE, PX, PX), np.float32)
    for view in range(2):
        k = np.arange(BE, dtype=np.float32)[:, None]
        position = np.arange(BE, dtype=np.float32)[None, :] + np.float32(SHEAR[view]) * (
            k - np.float32((BE - 1) / 2.0)
        )
        anchor = np.floor(position)
        fraction = (position - anchor).astype(np.float32)
        low = (np.float32(1.0) - fraction).astype(ml_dtypes.bfloat16).astype(np.float32)
        high = fraction.astype(ml_dtypes.bfloat16).astype(np.float32)
        anchor = anchor.astype(np.int32)
        along = cols if view == 0 else rows
        for tap, weight in ((0, low), (1, high)):
            source = anchor[:, along] + tap
            inside = (source >= 0) & (source < BE)
            for s in range(BE):
                index = (rows * BE + source[s]) if view == 0 else (source[s] * BE + cols)
                ok = inside[s]
                out[view, s, index[ok], cells[ok]] += weight[s, along][ok]
    return out.astype(ml_dtypes.bfloat16)


def encode(value):
    root = jnp.exp2(0.25 * jnp.log2(jnp.maximum(value, 1e-30)))
    code = jnp.minimum(root * TOP + 0.5, TOP).astype(jnp.int32) - 32768
    return code.astype(jnp.int16)


def decode(code):
    root = (code.astype(jnp.float32) + 32768.0) * (1.0 / TOP)
    square = root * root
    return square * square


def swap_rows_and_groups(block):
    row = lax.broadcasted_iota(jnp.int32, (8, 128), 0)
    group = lax.broadcasted_iota(jnp.int32, (8, 128), 1) // 16
    for bit in (1, 2, 4):
        row_bit = (row & bit) != 0
        group_bit = (group & bit) != 0
        from_below = pltpu.roll(pltpu.roll(block, 8 - bit, 0), 16 * bit, 1)
        from_above = pltpu.roll(pltpu.roll(block, bit, 0), 128 - 16 * bit, 1)
        moved = jnp.where(row_bit, from_above, from_below)
        block = jnp.where(row_bit == group_bit, block, moved)
    return block


def kernel(
    order_hbm, color_gain_hbm, color_bias_hbm, ext_gain_hbm, ext_bias_hbm, cost_hbm, bricks, cell_hbm, table_hbm, out,
    order, color_gain, color_bias, ext_gain, ext_bias, cost, raw, cell, near, table, sliced, samples, offset, slab, other, pair_out, *rest,
):
    pair_in = (rest[:NX], rest[NX:2 * NX])
    (
        staged, group, small_sem, raw_sem, table_sem, slab_send_sem, slab_recv_sem,
        pair_send_sem, pair_recv_sem, own_sem,
    ) = rest[2 * NX:]
    me = lax.axis_index("depth")
    x, y = me // NY, me % NY

    def chunk_copy(i):
        c = lax.rem(x + i + 1, NX)
        rows = pl.ds(pl.multiple_of(c * CHUNK * BE, CHUNK * BE), CHUNK * BE)
        return pltpu.make_async_copy(bricks.at[rows], raw.at[i], raw_sem.at[i])

    cell_copy = pltpu.make_async_copy(cell_hbm, cell, table_sem.at[0])
    table_copy = pltpu.make_async_copy(table_hbm, table, table_sem.at[1])

    small = [
        pltpu.make_async_copy(source, target, small_sem.at[n])
        for n, (source, target) in enumerate((
            (cost_hbm, cost), (order_hbm, order), (ext_gain_hbm, ext_gain), (ext_bias_hbm, ext_bias),
            (color_gain_hbm, color_gain), (color_bias_hbm, color_bias),
        ))
    ]
    for copy in small:
        copy.start()
    cell_copy.start()
    for i in range(NX):
        chunk_copy(i).start()
    table_copy.start()

    odd = lax.rem(y, 2)
    way = 2 * odd - 1
    partner = x * NY + y - way

    def peer(i, t):
        return lax.rem(x + i, NX) * NY + lax.rem(y + way * t + NY, NY)

    barrier = pltpu.get_barrier_semaphore()

    def greet(device):
        pl.semaphore_signal(barrier, inc=1, device_id={"depth": device}, device_id_type=MESH)

    for i in range(NX):
        for step in (0, -way, way, 2 * way, -2 * way, 3 * way):
            if i or not isinstance(step, int):
                greet(lax.rem(x + NX - i, NX) * NY + lax.rem(y + step + NY, NY))

    for copy in small:
        copy.wait()

    r = lax.broadcasted_iota(jnp.int32, (NB, NB), 0)
    q = lax.broadcasted_iota(jnp.int32, (NB, NB), 1)
    diagonal = jnp.where(r == q, (cost[...] * 4).astype(jnp.float32), 0.0).astype(jnp.bfloat16)
    level = jnp.dot(diagonal, jnp.ones((NB, 128), jnp.bfloat16), preferred_element_type=jnp.float32)
    gain = ext_gain[0] * LOG2E
    bias = ext_bias[0] * LOG2E + float(np.log2(LOG2E))
    for k in range(BE):
        offset[k] = jnp.where(k < level, bias, -1e9)
    regroup = jnp.where(q == (r % BE) * BE + r // BE, 1.0, 0.0).astype(jnp.bfloat16)

    masks = [order[v, 0] for v in range(2)]
    turned = [jnp.where(order[v, 0] > order[v, 31], 15, 0) for v in range(2)]
    half_gain = [color_gain[c] * 0.5 for c in range(3)]
    half_bias = [color_bias[c] * 0.5 for c in range(3)]

    slots = {0: 0, 7: 1, 1: 2, 6: 3, 2: 4, 3: 5}

    def to_partner(view, n):
        return pltpu.make_async_remote_copy(
            src_ref=slab.at[view, n, pl.ds(4, 2)], dst_ref=other.at[view, n],
            send_sem=slab_send_sem.at[view * NX + n], recv_sem=slab_recv_sem.at[view * NX + n],
            device_id={"depth": partner}, device_id_type=MESH,
        )

    def to_owner(view, n, u):
        sem = (view * NX + n) * 6 + slots[u]
        return pltpu.make_async_remote_copy(
            src_ref=pair_out.at[view, n, u - 2] if u in (2, 3) else slab.at[view, n, u],
            dst_ref=pair_in[view][n].at[slots[u]],
            send_sem=pair_send_sem.at[sem], recv_sem=pair_recv_sem.at[sem],
            device_id={"depth": peer(n + 1, u)}, device_id_type=MESH,
        )

    def own_copy(view):
        return pltpu.make_async_copy(
            slab.at[view, NX - 1, 0], pair_in[view][NX - 1].at[0], own_sem.at[view]
        )

    def regroup_chunk(i):
        chunk_copy(i).wait()
        for g in range(CHUNK // BE):
            lined = jnp.dot(
                regroup, raw[i, g * PX:(g + 1) * PX, :], preferred_element_type=jnp.float32
            ).astype(jnp.bfloat16)
            rows = pl.ds(pl.multiple_of(i * CHUNK + g * BE, BE), BE)
            for k in range(BE):
                for h in range(2):
                    sliced[k, h, rows, :] = lined[k * BE:(k + 1) * BE, h * 128:(h + 1) * 128]

    def resample_rows(view, first, count):
        def resample(k, carry):
            halves = [sliced[k, h, first:first + count] for h in range(2)]
            if view == 0:
                mixed = jnp.dot(
                    jnp.concatenate(halves, axis=0), near[k], preferred_element_type=jnp.float32
                )
                mixed = [mixed[:count], mixed[count:]]
            else:
                mixed = jnp.dot(
                    jnp.concatenate(halves, axis=1), table[k], preferred_element_type=jnp.float32
                )
                mixed = [mixed[:, :128], mixed[:, 128:]]
            for h in range(2):
                samples[view, k, h, first:first + count] = mixed[h]
            return carry

        lax.fori_loop(0, BE, resample, 0, unroll=16)

    def shade_part(view, n, first, end):
        c = lax.rem(x + n + 1, NX)

        def shade(pair, carry):
            places = []
            for e in range(2):
                u = pair * 2 + e
                row = lax.rem(y + way * u + NY, NY)
                g, h = row // 2, lax.rem(row, 2)
                places.append((
                    u, h, pl.ds(pl.multiple_of(n * CHUNK + g * BE, BE), BE),
                    pl.ds(pl.multiple_of(c * CHUNK + g * BE, BE), BE),
                ))
            depth = jnp.zeros((2 * BE, 128), jnp.float32)
            clear = jnp.ones((2 * BE, 128), jnp.float32)
            tints = [jnp.zeros((2 * BE, 128), jnp.float32) for _ in range(3)]
            for k in range(BE):
                kk = jnp.bitwise_xor(k, turned[view])
                s = jnp.concatenate([samples[view, kk, h, rows, :] for _, h, rows, _ in places], axis=0)
                b = jnp.concatenate([offset[kk, rows, :] for _, _, _, rows in places], axis=0)
                depth = depth - jnp.exp2(s * gain + b)
                after = jnp.exp2(depth)
                weight = clear - after
                clear = after
                for ch in range(3):
                    tints[ch] = tints[ch] + weight * jnp.tanh(s * half_gain[ch] + half_bias[ch])
            opaque = 1.0 - clear
            values = [0.5 * (opaque + t) for t in tints] + [opaque]
            for ch in range(4):
                code = encode(values[ch])
                for e in range(2):
                    slab[view, n, places[e][0], ch] = code[e * BE:(e + 1) * BE]
            return carry

        lax.fori_loop(first, end, shade, 0)

    def over(a, b, first):
        keep_a = jnp.where(first, 1.0, 1.0 - b[3])
        keep_b = jnp.where(first, 1.0 - a[3], 1.0)
        return [keep_a * a[ch] + keep_b * b[ch] for ch in range(4)]

    def mine_first(view):
        return (jnp.bitwise_xor(y, masks[view]) & 1) == 0

    def send_direct(view, n, us):
        for step in range(NX):

            def go(step=step):
                for u in us:
                    if u == 0 and step == NX - 1:
                        own_copy(view).start()
                    else:
                        to_owner(view, step, u).start()

            if isinstance(n, int):
                if n == step:
                    go()
            else:
                pl.when(n == step)(go)

    def send_slab(view, n):
        shade_part(view, n, 2, 4)
        if isinstance(n, int) and n == 0:
            pl.semaphore_wait(barrier, 6 * NX - 1)
        to_partner(view, n).start()
        send_direct(view, n, (7, 6))

    def finish_column(view, n):
        shade_part(view, n, 0, 2)
        to_partner(view, n).wait_recv()

        def one(e, carry):
            mine = [decode(slab[view, n, 2 + e, ch]) for ch in range(4)]
            theirs = [decode(other[view, n, 1 - e, ch]) for ch in range(4)]
            for ch, value in enumerate(over(mine, theirs, mine_first(view))):
                pair_out[view, n, e, ch] = encode(value)
            return carry

        lax.fori_loop(0, 2, one, 0)
        send_direct(view, n, (3, 2, 1, 0))

    def loop(start, body):
        def step(n, carry):
            body(n)
            return carry

        lax.fori_loop(start, NX, step, 0)

    group_of = lax.broadcasted_iota(jnp.int32, (BE, 128), 1) // BE
    keep = [jnp.where(group_of == i, 1.0, 0.0).astype(jnp.bfloat16) for i in range(8)]
    cell_copy.wait()

    def spread(k, carry):
        for i in range(8):
            near[k, i * BE:(i + 1) * BE, :] = cell[k] * keep[i]
        return carry

    lax.fori_loop(0, BE, spread, 0)
    regroup_chunk(0)
    resample_rows(0, 0, CHUNK)
    send_slab(0, 0)
    loop(1, regroup_chunk)
    resample_rows(0, CHUNK, NB - CHUNK)
    loop(1, lambda n: send_slab(0, n))
    table_copy.wait()
    resample_rows(1, 0, NB)

    def both(n):
        shade_part(1, n, 2, 3)
        to_partner(1, n).start()
        finish_column(0, n)

    loop(0, both)

    def last(n):
        finish_column(1, n)
        shade_part(1, n, 3, 4)
        send_direct(1, n, (7, 6))

    loop(0, last)

    for view in range(2):
        for n in range(NX):
            for u in slots:
                if u == 0 and n == NX - 1:
                    own_copy(view).wait()
                else:
                    to_owner(view, n, u).wait_recv()
            raw_slabs = [[decode(pair_in[view][n][e, ch]) for ch in range(4)] for e in range(4)]
            first = mine_first(view)
            pairs = [over(raw_slabs[0], raw_slabs[1], first), over(raw_slabs[3], raw_slabs[2], first)]
            pairs += [[decode(pair_in[view][n][e, ch]) for ch in range(4)] for e in (4, 5)]
            for t in range(4):
                for ch in range(4):
                    staged[t, ch] = pairs[t][ch]
            clear = jnp.ones((BE, 128), jnp.float32)
            total = [jnp.zeros((BE, 128), jnp.float32) for _ in range(4)]
            for rank in range(4):
                pair = jnp.bitwise_xor(rank, (masks[view] // 2) & 3)
                delta = (way * (pair - y // 2)) & 3
                t = jnp.bitwise_xor(delta, delta // 2)
                for ch in range(4):
                    total[ch] = total[ch] + clear * staged[t, ch]
                clear = 1.0 - total[3]
            for ch in range(4):
                group[view, n, ch] = total[ch]

        clear = jnp.ones((BE, 128), jnp.float32)
        total = [jnp.zeros((BE, 128), jnp.float32) for _ in range(4)]
        for rank in range(NX):
            source = jnp.bitwise_xor(rank, masks[view] // NY)
            n = (x - source - 1) & (NX - 1)
            for ch in range(4):
                total[ch] = total[ch] + clear * group[view, n, ch]
            clear = 1.0 - total[3]
        for ch in range(4):
            for h in range(2):
                out[view, ch, :, h * 128:(h + 1) * 128] = swap_rows_and_groups(total[ch][h * 8:(h + 1) * 8, :])

    for view in range(2):
        for n in range(NX):
            to_partner(view, n).wait_send()
            for u in slots:
                if u or n < NX - 1:
                    to_owner(view, n, u).wait_send()


def shards(bricks, cost, order, color_gain, color_bias, ext_gain, ext_bias):
    tables = shear_table()
    cell = jnp.asarray(np.tile(tables[0, :, :BE, :BE], (1, 1, 8)))
    table = jnp.asarray(tables[1])
    vmem = pl.BlockSpec(memory_space=pltpu.VMEM)

    def hbm(array):
        return pltpu.with_memory_space_constraint(array, pltpu.HBM)

    anywhere = pl.BlockSpec(memory_space=pltpu.HBM)
    return pl.pallas_call(
        kernel,
        out_shape=jax.ShapeDtypeStruct((2, 4, 8, 256), jnp.float32),
        in_specs=[anywhere] * 9,
        out_specs=vmem,
        scratch_shapes=[
            pltpu.SMEM((2, 32), jnp.int32),
            pltpu.SMEM((3,), jnp.float32),
            pltpu.SMEM((3,), jnp.float32),
            pltpu.SMEM((1,), jnp.float32),
            pltpu.SMEM((1,), jnp.float32),
            pltpu.VMEM((1, NB), jnp.int32),
            pltpu.VMEM((NX, CHUNK * BE, PX), jnp.bfloat16),
            pltpu.VMEM((BE, BE, 128), jnp.bfloat16),
            pltpu.VMEM((BE, 128, 128), jnp.bfloat16),
            pltpu.VMEM((BE, PX, PX), jnp.bfloat16),
            pltpu.VMEM((BE, 2, NB, 128), jnp.bfloat16),
            pltpu.VMEM((2, BE, 2, NB, 128), jnp.float32),
            pltpu.VMEM((BE, NB, 128), jnp.float32),
            pltpu.VMEM((2, NX, 8, 4, BE, 128), jnp.int16),
            pltpu.VMEM((2, NX, 2, 4, BE, 128), jnp.int16),
            pltpu.VMEM((2, NX, 2, 4, BE, 128), jnp.int16),
            *[pltpu.VMEM((6, 4, BE, 128), jnp.int16) for _ in range(2 * NX)],
            pltpu.VMEM((4, 4, BE, 128), jnp.float32),
            pltpu.VMEM((2, NX, 4, BE, 128), jnp.float32),
            pltpu.SemaphoreType.DMA((6,)),
            pltpu.SemaphoreType.DMA((NX,)),
            pltpu.SemaphoreType.DMA((2,)),
            pltpu.SemaphoreType.DMA((NX * 2,)),
            pltpu.SemaphoreType.DMA((NX * 2,)),
            pltpu.SemaphoreType.DMA((2 * NX * 6,)),
            pltpu.SemaphoreType.DMA((2 * NX * 6,)),
            pltpu.SemaphoreType.DMA((2,)),
        ],
        compiler_params=pltpu.CompilerParams(
            collective_id=0, has_side_effects=True, vmem_limit_bytes=48 * 2**20
        ),
    )(hbm(order), hbm(color_gain), hbm(color_bias), ext_gain, ext_bias, hbm(cost), hbm(bricks.reshape(NB * BE, PX)), hbm(cell), hbm(table))


def solution(mesh):
    in_specs = (P("depth", "image", None, None), P("depth", "image"), P(), P(), P(), P(), P())
    out_specs = P(None, None, "depth", "image")
    return jax.shard_map(shards, mesh=mesh, in_specs=in_specs, out_specs=out_specs, check_vma=False)
```

```python
import jax
import jax.numpy as jnp
import numpy as np
import ml_dtypes
from jax import lax
from jax.experimental import pallas as pl
from jax.experimental.pallas import tpu as pltpu
from jax.sharding import PartitionSpec as P

BE = 16
PX = BE * BE
NB = 256
NX = 4
NY = 8
CHUNK = NB // NX
SHEAR = (0.45, -0.3)
LOG2E = 1.4426950408889634
TOP = 65535.0
MESH = pl.DeviceIdType.MESH


def shear_table():
    cells = np.arange(PX)
    rows, cols = cells // BE, cells % BE
    out = np.zeros((2, BE, PX, PX), np.float32)
    for view in range(2):
        k = np.arange(BE, dtype=np.float32)[:, None]
        position = np.arange(BE, dtype=np.float32)[None, :] + np.float32(SHEAR[view]) * (
            k - np.float32((BE - 1) / 2.0)
        )
        anchor = np.floor(position)
        fraction = (position - anchor).astype(np.float32)
        low = (np.float32(1.0) - fraction).astype(ml_dtypes.bfloat16).astype(np.float32)
        high = fraction.astype(ml_dtypes.bfloat16).astype(np.float32)
        anchor = anchor.astype(np.int32)
        along = cols if view == 0 else rows
        for tap, weight in ((0, low), (1, high)):
            source = anchor[:, along] + tap
            inside = (source >= 0) & (source < BE)
            for s in range(BE):
                index = (rows * BE + source[s]) if view == 0 else (source[s] * BE + cols)
                ok = inside[s]
                out[view, s, index[ok], cells[ok]] += weight[s, along][ok]
    return out.astype(ml_dtypes.bfloat16)


def encode(value):
    root = jnp.exp2(0.25 * jnp.log2(jnp.maximum(value, 1e-30)))
    code = jnp.minimum(root * TOP + 0.5, TOP).astype(jnp.int32) - 32768
    return code.astype(jnp.int16)


def decode(code):
    root = (code.astype(jnp.float32) + 32768.0) * (1.0 / TOP)
    square = root * root
    return square * square


def swap_rows_and_groups(block):
    row = lax.broadcasted_iota(jnp.int32, (8, 128), 0)
    group = lax.broadcasted_iota(jnp.int32, (8, 128), 1) // 16
    for bit in (1, 2, 4):
        row_bit = (row & bit) != 0
        group_bit = (group & bit) != 0
        from_below = pltpu.roll(pltpu.roll(block, 8 - bit, 0), 16 * bit, 1)
        from_above = pltpu.roll(pltpu.roll(block, bit, 0), 128 - 16 * bit, 1)
        moved = jnp.where(row_bit, from_above, from_below)
        block = jnp.where(row_bit == group_bit, block, moved)
    return block


def kernel(
    order_hbm, color_gain_hbm, color_bias_hbm, ext_gain_hbm, ext_bias_hbm, cost_hbm, bricks, cell_hbm, table_hbm, out,
    order, color_gain, color_bias, ext_gain, ext_bias, cost, raw, cell, near, table, sliced, samples, offset, slab, other, pair_out, *rest,
):
    pair_in = (rest[:NX], rest[NX:2 * NX])
    (
        staged, group, small_sem, raw_sem, table_sem, slab_send_sem, slab_recv_sem,
        pair_send_sem, pair_recv_sem, own_sem,
    ) = rest[2 * NX:]
    me = lax.axis_index("depth")
    x, y = me // NY, me % NY

    def chunk_copy(i):
        c = lax.rem(x + i + 1, NX)
        rows = pl.ds(pl.multiple_of(c * CHUNK * BE, CHUNK * BE), CHUNK * BE)
        return pltpu.make_async_copy(bricks.at[rows], raw.at[i], raw_sem.at[i])

    cell_copy = pltpu.make_async_copy(cell_hbm, cell, table_sem.at[0])
    table_copy = pltpu.make_async_copy(table_hbm, table, table_sem.at[1])

    small = [
        pltpu.make_async_copy(source, target, small_sem.at[n])
        for n, (source, target) in enumerate((
            (cost_hbm, cost), (order_hbm, order), (ext_gain_hbm, ext_gain), (ext_bias_hbm, ext_bias),
            (color_gain_hbm, color_gain), (color_bias_hbm, color_bias),
        ))
    ]
    for copy in small:
        copy.start()
    cell_copy.start()
    for i in range(NX):
        chunk_copy(i).start()
    table_copy.start()

    odd = lax.rem(y, 2)
    way = 2 * odd - 1
    partner = x * NY + y - way

    def peer(i, t):
        return lax.rem(x + i, NX) * NY + lax.rem(y + way * t + NY, NY)

    barrier = pltpu.get_barrier_semaphore()

    def greet(device):
        pl.semaphore_signal(barrier, inc=1, device_id={"depth": device}, device_id_type=MESH)

    for i in range(NX):
        for step in (0, -way, way, 2 * way, -2 * way, 3 * way):
            if i or not isinstance(step, int):
                greet(lax.rem(x + NX - i, NX) * NY + lax.rem(y + step + NY, NY))

    for copy in small:
        copy.wait()
    cell_copy.wait()
    chunk_copy(0).wait()

    r = lax.broadcasted_iota(jnp.int32, (NB, NB), 0)
    q = lax.broadcasted_iota(jnp.int32, (NB, NB), 1)
    diagonal = jnp.where(r == q, (cost[...] * 4).astype(jnp.float32), 0.0).astype(jnp.bfloat16)
    level = jnp.dot(diagonal, jnp.ones((NB, 128), jnp.bfloat16), preferred_element_type=jnp.float32)
    gain = ext_gain[0] * LOG2E
    bias = ext_bias[0] * LOG2E + float(np.log2(LOG2E))
    regroup = jnp.where(q == (r % BE) * BE + r // BE, 1.0, 0.0).astype(jnp.bfloat16)

    masks = [order[v, 0] for v in range(2)]
    turned = [jnp.where(order[v, 0] > order[v, 31], 15, 0) for v in range(2)]

    def set_offset(view):
        for k in range(BE):
            kk = jnp.bitwise_xor(k, turned[view]).astype(jnp.float32)
            offset[view, k] = jnp.where(kk < level, bias, -1e9)

    half_gain = [color_gain[c] * 0.5 for c in range(3)]
    half_bias = [color_bias[c] * 0.5 for c in range(3)]

    slots = {0: 0, 7: 1, 1: 2, 6: 3, 2: 4, 3: 5}

    def to_partner(view, n):
        return pltpu.make_async_remote_copy(
            src_ref=slab.at[view, n, pl.ds(4, 2)], dst_ref=other.at[view, n],
            send_sem=slab_send_sem.at[view * NX + n], recv_sem=slab_recv_sem.at[view * NX + n],
            device_id={"depth": partner}, device_id_type=MESH,
        )

    def to_owner(view, n, u):
        sem = (view * NX + n) * 6 + slots[u]
        return pltpu.make_async_remote_copy(
            src_ref=pair_out.at[view, n, u - 2] if u in (2, 3) else slab.at[view, n, u],
            dst_ref=pair_in[view][n].at[slots[u]],
            send_sem=pair_send_sem.at[sem], recv_sem=pair_recv_sem.at[sem],
            device_id={"depth": peer(n + 1, u)}, device_id_type=MESH,
        )

    def own_copy(view):
        return pltpu.make_async_copy(
            slab.at[view, NX - 1, 0], pair_in[view][NX - 1].at[0], own_sem.at[view]
        )

    def regroup_chunk(i):
        if not isinstance(i, int):
            chunk_copy(i).wait()
        for g in range(CHUNK // BE):
            lined = jnp.dot(
                regroup, raw[i, g * PX:(g + 1) * PX, :], preferred_element_type=jnp.float32
            ).astype(jnp.bfloat16)
            rows = pl.ds(pl.multiple_of(i * CHUNK + g * BE, BE), BE)
            for k in range(BE):
                for h in range(2):
                    sliced[k, h, rows, :] = lined[k * BE:(k + 1) * BE, h * 128:(h + 1) * 128]

    def resample_rows(view, first, count):
        def resample(k, carry):
            kk = jnp.bitwise_xor(k, turned[view])
            halves = [sliced[kk, h, first:first + count] for h in range(2)]
            if view == 0:
                mixed = jnp.dot(
                    jnp.concatenate(halves, axis=0), near[kk], preferred_element_type=jnp.float32
                )
                mixed = [mixed[:count], mixed[count:]]
            else:
                mixed = jnp.dot(
                    jnp.concatenate(halves, axis=1), table[kk], preferred_element_type=jnp.float32
                )
                mixed = [mixed[:, :128], mixed[:, 128:]]
            for h in range(2):
                samples[view, k, h, first:first + count] = mixed[h]
            return carry

        lax.fori_loop(0, BE, resample, 0, unroll=16)

    def shade_part(view, n, first, end):
        c = lax.rem(x + n + 1, NX)

        def shade(pair, carry):
            places = []
            for e in range(2):
                u = pair * 2 + e
                row = lax.rem(y + way * u + NY, NY)
                g, h = row // 2, lax.rem(row, 2)
                places.append((
                    u, h, pl.ds(pl.multiple_of(n * CHUNK + g * BE, BE), BE),
                    pl.ds(pl.multiple_of(c * CHUNK + g * BE, BE), BE),
                ))
            depth = jnp.zeros((2 * BE, 128), jnp.float32)
            clear = jnp.ones((2 * BE, 128), jnp.float32)
            tints = [jnp.zeros((2 * BE, 128), jnp.float32) for _ in range(3)]
            for k in range(BE):
                s = jnp.concatenate([samples[view, k, h, rows, :] for _, h, rows, _ in places], axis=0)
                b = jnp.concatenate([offset[view, k, rows, :] for _, _, _, rows in places], axis=0)
                depth = depth - jnp.exp2(s * gain + b)
                after = jnp.exp2(depth)
                weight = clear - after
                clear = after
                for ch in range(3):
                    tints[ch] = tints[ch] + weight * jnp.tanh(s * half_gain[ch] + half_bias[ch])
            opaque = 1.0 - clear
            values = [0.5 * (opaque + t) for t in tints] + [opaque]
            for ch in range(4):
                code = encode(values[ch])
                for e in range(2):
                    slab[view, n, places[e][0], ch] = code[e * BE:(e + 1) * BE]
            return carry

        lax.fori_loop(first, end, shade, 0)

    def over(a, b, first):
        keep_a = jnp.where(first, 1.0, 1.0 - b[3])
        keep_b = jnp.where(first, 1.0 - a[3], 1.0)
        return [keep_a * a[ch] + keep_b * b[ch] for ch in range(4)]

    def mine_first(view):
        return (jnp.bitwise_xor(y, masks[view]) & 1) == 0

    def send_direct(view, n, us):
        for step in range(NX):

            def go(step=step):
                for u in us:
                    if u == 0 and step == NX - 1:
                        own_copy(view).start()
                    else:
                        to_owner(view, step, u).start()

            if isinstance(n, int):
                if n == step:
                    go()
            else:
                pl.when(n == step)(go)

    def send_slab(view, n):
        shade_part(view, n, 2, 4)
        to_partner(view, n).start()
        send_direct(view, n, (7, 6))

    def finish_column(view, n):
        shade_part(view, n, 1, 2)
        to_partner(view, n).wait_recv()

        def one(e, carry):
            mine = [decode(slab[view, n, 2 + e, ch]) for ch in range(4)]
            theirs = [decode(other[view, n, 1 - e, ch]) for ch in range(4)]
            for ch, value in enumerate(over(mine, theirs, mine_first(view))):
                pair_out[view, n, e, ch] = encode(value)
            return carry

        lax.fori_loop(0, 2, one, 0)
        send_direct(view, n, (3, 2))
        shade_part(view, n, 0, 1)
        send_direct(view, n, (1, 0))

    def loop(start, body):
        def step(n, carry):
            body(n)
            return carry

        lax.fori_loop(start, NX, step, 0)

    group_of = lax.broadcasted_iota(jnp.int32, (BE, 128), 1) // BE
    keep = [jnp.where(group_of == i, 1.0, 0.0).astype(jnp.bfloat16) for i in range(8)]

    def spread(k, carry):
        for i in range(8):
            near[k, i * BE:(i + 1) * BE, :] = cell[k] * keep[i]
        return carry

    lax.fori_loop(0, BE, spread, 0, unroll=16)
    regroup_chunk(0)
    set_offset(0)
    resample_rows(0, 0, CHUNK)
    shade_part(0, 0, 2, 4)
    set_offset(1)
    loop(1, regroup_chunk)
    resample_rows(0, CHUNK, NB - CHUNK)
    pl.semaphore_wait(barrier, 6 * NX - 1)
    to_partner(0, 0).start()
    send_direct(0, 0, (7, 6))
    def early(n):
        shade_part(0, n, 2, 3)
        to_partner(0, n).start()
        shade_part(0, n, 3, 4)
        send_direct(0, n, (7, 6))

    loop(1, early)
    table_copy.wait()
    resample_rows(1, 0, NB)

    def both(n):
        shade_part(1, n, 2, 3)
        to_partner(1, n).start()
        finish_column(0, n)

    loop(0, both)

    def last(n):
        finish_column(1, n)
        shade_part(1, n, 3, 4)
        send_direct(1, n, (7, 6))

    loop(0, last)

    for view in range(2):
        for n in range(NX):
            for u in slots:
                if u == 0 and n == NX - 1:
                    own_copy(view).wait()
                else:
                    to_owner(view, n, u).wait_recv()
            raw_slabs = [[decode(pair_in[view][n][e, ch]) for ch in range(4)] for e in range(4)]
            first = mine_first(view)
            pairs = [over(raw_slabs[0], raw_slabs[1], first), over(raw_slabs[3], raw_slabs[2], first)]
            pairs += [[decode(pair_in[view][n][e, ch]) for ch in range(4)] for e in (4, 5)]
            for t in range(4):
                for ch in range(4):
                    staged[t, ch] = pairs[t][ch]
            clear = jnp.ones((BE, 128), jnp.float32)
            total = [jnp.zeros((BE, 128), jnp.float32) for _ in range(4)]
            for rank in range(4):
                pair = jnp.bitwise_xor(rank, (masks[view] // 2) & 3)
                delta = (way * (pair - y // 2)) & 3
                t = jnp.bitwise_xor(delta, delta // 2)
                for ch in range(4):
                    total[ch] = total[ch] + clear * staged[t, ch]
                clear = 1.0 - total[3]
            for ch in range(4):
                group[view, n, ch] = total[ch]

        clear = jnp.ones((BE, 128), jnp.float32)
        total = [jnp.zeros((BE, 128), jnp.float32) for _ in range(4)]
        for rank in range(NX):
            source = jnp.bitwise_xor(rank, masks[view] // NY)
            n = (x - source - 1) & (NX - 1)
            for ch in range(4):
                total[ch] = total[ch] + clear * group[view, n, ch]
            clear = 1.0 - total[3]
        for ch in range(4):
            for h in range(2):
                out[view, ch, :, h * 128:(h + 1) * 128] = swap_rows_and_groups(total[ch][h * 8:(h + 1) * 8, :])

    for view in range(2):
        for n in range(NX):
            to_partner(view, n).wait_send()
            for u in slots:
                if u or n < NX - 1:
                    to_owner(view, n, u).wait_send()


def shards(bricks, cost, order, color_gain, color_bias, ext_gain, ext_bias):
    tables = shear_table()
    cell = jnp.asarray(np.tile(tables[0, :, :BE, :BE], (1, 1, 8)))
    table = jnp.asarray(tables[1])
    vmem = pl.BlockSpec(memory_space=pltpu.VMEM)

    def hbm(array):
        return pltpu.with_memory_space_constraint(array, pltpu.HBM)

    anywhere = pl.BlockSpec(memory_space=pltpu.HBM)
    return pl.pallas_call(
        kernel,
        out_shape=jax.ShapeDtypeStruct((2, 4, 8, 256), jnp.float32),
        in_specs=[anywhere] * 9,
        out_specs=vmem,
        scratch_shapes=[
            pltpu.SMEM((2, 32), jnp.int32),
            pltpu.SMEM((3,), jnp.float32),
            pltpu.SMEM((3,), jnp.float32),
            pltpu.SMEM((1,), jnp.float32),
            pltpu.SMEM((1,), jnp.float32),
            pltpu.VMEM((1, NB), jnp.int32),
            pltpu.VMEM((NX, CHUNK * BE, PX), jnp.bfloat16),
            pltpu.VMEM((BE, BE, 128), jnp.bfloat16),
            pltpu.VMEM((BE, 128, 128), jnp.bfloat16),
            pltpu.VMEM((BE, PX, PX), jnp.bfloat16),
            pltpu.VMEM((BE, 2, NB, 128), jnp.bfloat16),
            pltpu.VMEM((2, BE, 2, NB, 128), jnp.float32),
            pltpu.VMEM((2, BE, NB, 128), jnp.float32),
            pltpu.VMEM((2, NX, 8, 4, BE, 128), jnp.int16),
            pltpu.VMEM((2, NX, 2, 4, BE, 128), jnp.int16),
            pltpu.VMEM((2, NX, 2, 4, BE, 128), jnp.int16),
            *[pltpu.VMEM((6, 4, BE, 128), jnp.int16) for _ in range(2 * NX)],
            pltpu.VMEM((4, 4, BE, 128), jnp.float32),
            pltpu.VMEM((2, NX, 4, BE, 128), jnp.float32),
            pltpu.SemaphoreType.DMA((6,)),
            pltpu.SemaphoreType.DMA((NX,)),
            pltpu.SemaphoreType.DMA((2,)),
            pltpu.SemaphoreType.DMA((NX * 2,)),
            pltpu.SemaphoreType.DMA((NX * 2,)),
            pltpu.SemaphoreType.DMA((2 * NX * 6,)),
            pltpu.SemaphoreType.DMA((2 * NX * 6,)),
            pltpu.SemaphoreType.DMA((2,)),
        ],
        compiler_params=pltpu.CompilerParams(
            collective_id=0, has_side_effects=True, vmem_limit_bytes=48 * 2**20
        ),
    )(hbm(order), hbm(color_gain), hbm(color_bias), ext_gain, ext_bias, hbm(cost), hbm(bricks.reshape(NB * BE, PX)), hbm(cell), hbm(table))


def solution(mesh):
    in_specs = (P("depth", "image", None, None), P("depth", "image"), P(), P(), P(), P(), P())
    out_specs = P(None, None, "depth", "image")
    return jax.shard_map(shards, mesh=mesh, in_specs=in_specs, out_specs=out_specs, check_vma=False)
```
